32 devices in a mesh: energy: 8 (over z, core), momentum: 4 (over y, x).
Axes of the slice: x: 2, y: 2, z: 4, core: 2. Of those that a mesh axis runs over, the one named last changes fastest.
Arguments:
- green: bfloat16 [24, 4, 2, 384, 384], P('energy', 'momentum'), may hold values from -0.3125 to 0.3125
- contact: bfloat16 [24, 4, 2, 3, 128, 128], P('energy', 'momentum'), may hold values from -6 to 6
- tile_count: int32 [24], P('energy'), may hold values from 1 to 3
- offsets: int32 [3], replicated, may hold values from 1 to 3, as said below
- pair_index: int32 [3, 4, 4], replicated, may hold values from 0 to 15
- coupling_table: float32 [3, 16], replicated, may hold values from 0.05 to 0.3
Outputs:
- lesser_tiles: bfloat16 [24, 4, 2, 3, 128, 128], P('energy', 'momentum')
- self_energy: bfloat16 [24, 4, 2, 3, 128, 128], P('energy', 'momentum')
The draws below stay inside these ranges and needn't reach their ends.
Inputs may be any that keep to these rules, and one draw needn't show every extreme that they name: `offsets`: the largest offset equals 3 in every draw.
All inputs are finite; a program needn't handle non-finite values.
Results may differ from the reference program's by a relative error of at most 0.009.
Values may be sent and summed in bfloat16 or wider, within the bound.
A program may use at most 64 MiB of HBM per device.

```python
import math
import jax
import jax.numpy as jnp
from jax import lax

TILE = 128
NT = 3
B = 384
OMAX = 3
NMODE = 3
NC = 16
ITERS = 2
NE = 24
NK = 4


def draw_offsets(key, part):
    first, second = jax.random.split(jax.random.fold_in(key, 17))
    values = jax.random.randint(first, (NMODE,), 1, OMAX + 1).astype(jnp.int32)
    where = jax.random.randint(second, (), 0, NMODE).astype(jnp.int32)
    modes = jnp.arange(NMODE, dtype=jnp.int32)
    return jnp.where(modes == where, jnp.int32(OMAX), values).astype(jnp.int32)


def place_ends(entries, stream_key, smallest, top_value):
    index_at = [jax.random.randint(jax.random.fold_in(stream_key, axis), (), 0, length) for axis, length in enumerate(entries.shape)]
    widest = entries.shape.index(max(entries.shape))
    neighbour = index_at[:widest] + [(index_at[widest] + 1) % entries.shape[widest]] + index_at[widest + 1:]
    return entries.at[tuple(index_at)].set(smallest).at[tuple(neighbour)].set(top_value)


def level_of(own_key, dims, shards, low, top_value):
    def one(axis_at, shards_of):
        heights = jax.random.uniform(jax.random.fold_in(jax.random.fold_in(own_key, 6), axis_at), (shards_of,), jnp.float32, low / len(shards), top_value / len(shards))
        return jnp.repeat(jnp.exp(heights), dims[axis_at] // shards_of).reshape((-1,) + (1,) * (len(dims) - axis_at - 1))

    gain = one(*shards[0])
    for cut in shards[1:]:
        gain = gain * one(*cut)
    return gain


def noise(stream_key, shape, spread, reach, pieces=(), kind=jnp.bfloat16):
    result = jax.random.normal(stream_key, shape, jnp.float32) * spread
    if len(pieces) > 0:
        result = level_of(stream_key, shape, pieces, -0.22, 0.18) * result
    return jnp.clip(result, min=-reach, max=reach).astype(kind)


def setup_inputs(seed: int = 0) -> dict:
    keys = jax.random.split(jax.random.key(seed), 7)
    return {
        "green": noise(keys[0], (NE, NK, 2, B, B), B ** -0.5, 0.3125, ((0, 8), (1, 4))),
        "contact": noise(keys[1], (NE, NK, 2, NT, TILE, TILE), 1.0, 6.0, ((0, 8), (1, 4))),
        "tile_count": place_ends(jax.random.randint(keys[2], (NE,), 1, NT + 1), jax.random.fold_in(keys[2], 1), 1, NT).astype(jnp.int32),
        "offsets": draw_offsets(jax.random.fold_in(keys[6], 71), 0),
        "pair_index": place_ends(jax.random.randint(keys[4], (NMODE, NK, NK), 0, NC), jax.random.fold_in(keys[4], 1), 0, NC - 1).astype(jnp.int32),
        "coupling_table": jnp.clip(jnp.exp(jax.random.uniform(keys[5], (NMODE, NC), jnp.float32, math.log(0.05), math.log(0.3))), 0.05, 0.3),
    }


def couplings(pair_index, coupling_table):
    hits = (pair_index[..., None] == jnp.arange(NC, dtype=jnp.int32)).astype(jnp.float32)
    return jnp.einsum("mkqc,mc->mkq", hits, coupling_table, precision=lax.Precision.HIGHEST)


def lesser_point(block, sigma, count):
    g_real = block[0].reshape(B, NT, TILE).astype(jnp.float32)
    g_imag = block[1].reshape(B, NT, TILE).astype(jnp.float32)
    s_real = sigma[0].astype(jnp.float32)
    s_imag = sigma[1].astype(jnp.float32)
    polarization_real = jnp.einsum("rtc,tcd->rtd", g_real, s_real) - jnp.einsum("rtc,tcd->rtd", g_imag, s_imag)
    polarization_imag = jnp.einsum("rtc,tcd->rtd", g_real, s_imag) + jnp.einsum("rtc,tcd->rtd", g_imag, s_real)
    polarization_real = polarization_real.astype(jnp.bfloat16).astype(jnp.float32).reshape(NT, TILE, B)
    polarization_imag = polarization_imag.astype(jnp.bfloat16).astype(jnp.float32).reshape(NT, TILE, B)
    hamiltonian_real = block[0].astype(jnp.float32).reshape(NT, TILE, B)
    hamiltonian_imag = block[1].astype(jnp.float32).reshape(NT, TILE, B)
    phonon_propagator_real = jnp.einsum("neg,nig->nei", polarization_real, hamiltonian_real) + jnp.einsum("neg,nig->nei", polarization_imag, hamiltonian_imag)
    phonon_propagator_imag = jnp.einsum("neg,nig->nei", polarization_imag, hamiltonian_real) - jnp.einsum("neg,nig->nei", polarization_real, hamiltonian_imag)
    live = (jnp.arange(NT, dtype=jnp.int32) < count).astype(jnp.float32)[:, None, None]
    return jnp.stack([phonon_propagator_real * live, phonon_propagator_imag * live]).astype(jnp.bfloat16)


def reference(green, contact, tile_count, offsets, pair_index, coupling_table):
    coupling = couplings(pair_index, coupling_table)
    sigma = contact
    lesser = contact
    for sweep in range(ITERS):
        def one_energy(items):
            blocks, sigmas, count = items
            return jax.vmap(lambda blk, sig: lesser_point(blk, sig, count))(blocks, sigmas)
        lesser = lax.map(one_energy, (green, sigma, tile_count))
        wide = lesser.astype(jnp.float32)
        total = contact.astype(jnp.float32)
        for phonon_mode in range(NMODE):
            mixed = jnp.einsum("kq,eqabcd->ekabcd", coupling[phonon_mode], wide, precision=lax.Precision.HIGHEST)
            padded = jnp.pad(mixed, ((OMAX, OMAX), (0, 0), (0, 0), (0, 0), (0, 0), (0, 0)))
            shift = offsets[phonon_mode].astype(jnp.int32)
            lower = lax.dynamic_slice_in_dim(padded, (OMAX - shift).astype(jnp.int32), NE, 0)
            upper = lax.dynamic_slice_in_dim(padded, (OMAX + shift).astype(jnp.int32), NE, 0)
            total = total + (lower + upper)
        sigma = total.astype(jnp.bfloat16)
    return lesser, sigma
```

```python
import functools

import jax
import jax.numpy as jnp
from jax import lax
from jax.experimental import pallas as pl
from jax.experimental.pallas import tpu as pltpu
from jax.sharding import PartitionSpec as P

OMAX = 3
ITERS = 2
PACK = 16
CHUNKS = 3
MESH = pl.DeviceIdType.MESH


def born(ne, nk, chunks, green, contact, counts, offsets, pairs, table, lesser_out, sigma_out,
         g, start, product, lesser, band, mixed, back, sigma, weights,
         in_sem, own_sem, out_sem, a_send, a_recv, h_send, h_recv, b_send, b_recv):
    energies, order = g.shape[0], g.shape[-1]
    tile = start.shape[-1]
    tiles = order // tile
    rows = band.shape[4]
    part = rows // chunks
    modes = offsets.shape[0]
    e, me = lax.axis_index("energy"), lax.axis_index("momentum")
    has_left, has_right = e > 0, e < ne - 1
    left, right = jnp.maximum(e - 1, 0), jnp.minimum(e + 1, ne - 1)

    loads = [pltpu.make_async_copy(contact, start, in_sem.at[energies])]
    loads += [pltpu.make_async_copy(green.at[i], g.at[i], in_sem.at[i]) for i in range(energies)]
    for load in loads:
        load.start()

    def peer(j):
        return lax.rem(me + j, nk)

    barrier = pltpu.get_barrier_semaphore()
    for j in range(1, nk):
        pl.semaphore_signal(barrier, inc=1, device_id={"momentum": peer(j)}, device_id_type=MESH)

    @pl.when(has_left)
    def _():
        pl.semaphore_signal(barrier, inc=1, device_id={"energy": left}, device_id_type=MESH)

    @pl.when(has_right)
    def _():
        pl.semaphore_signal(barrier, inc=1, device_id={"energy": right}, device_id_type=MESH)

    def weigh(i, carry):
        k, q = i // nk, i % nk
        sums = [jnp.float32(0)] * OMAX
        for m in range(modes):
            value = table[m, pairs[m, k, q]]
            for d in range(OMAX):
                sums[d] = sums[d] + jnp.where(offsets[m] == d + 1, value, jnp.float32(0))
        for d in range(OMAX):
            weights[d, k, q] = jnp.full(weights.shape[3:], sums[d], jnp.float32)
        return carry

    lax.fori_loop(0, nk * nk, weigh, 0)

    def clear(side):
        for it in range(ITERS):
            for i in range(energies):
                def zero(q, carry):
                    band[it, side, i, q] = jnp.zeros(band.shape[4:], band.dtype)
                    return carry
                lax.fori_loop(0, nk, zero, 0)

    @pl.when(e == 0)
    def _():
        clear(0)

    @pl.when(e == ne - 1)
    def _():
        clear(2)

    def onsite(it, i, source):
        for t in range(tiles):
            cols = slice(t * tile, (t + 1) * tile)
            s_real = source[i, t * tile:(t + 1) * tile, :]
            s_imag = source[i, (tiles + t) * tile:(tiles + t + 1) * tile, :]
            s = jnp.concatenate([jnp.concatenate([s_real, s_imag], 1),
                                 jnp.concatenate([-s_imag, s_real], 1)], 0)
            a = jnp.concatenate([g[i, 0, :, cols], g[i, 1, :, cols]], 1)
            p = jnp.dot(a, s, preferred_element_type=jnp.float32).astype(jnp.bfloat16)
            product[0, :, cols] = p[:, :tile]
            product[1, :, cols] = p[:, tile:]
        for t in range(tiles):
            r = slice(t * tile, (t + 1) * tile)
            p = jnp.concatenate([product[0, r, :], product[1, r, :]], 0)
            h = jnp.concatenate([g[i, 0, r, :], g[i, 1, r, :]], 0)
            o = lax.dot_general(p, h, (((1,), (1,)), ((), ())), preferred_element_type=jnp.float32)
            live = jnp.where(t < counts[i], jnp.float32(1), jnp.float32(0))
            real = (o[:tile, :tile] + o[tile:, tile:]) * live
            imag = (o[tile:, :tile] - o[:tile, tile:]) * live
            lesser[it, i, t * tile:(t + 1) * tile, :] = real.astype(jnp.bfloat16)
            lesser[it, i, (tiles + t) * tile:(tiles + t + 1) * tile, :] = imag.astype(jnp.bfloat16)

    def span(owner, c):
        return pl.ds(pl.multiple_of(owner * rows + c * part, PACK), part)

    def outward(it, c, j):
        return pltpu.make_async_remote_copy(
            src_ref=lesser.at[it, :, span(peer(j), c), :],
            dst_ref=band.at[it, 1, :, me, pl.ds(c * part, part), :],
            send_sem=a_send.at[it, c, j], recv_sem=a_recv.at[it, c, j],
            device_id={"momentum": peer(j)}, device_id_type=MESH)

    def halo(it, c, side):
        return pltpu.make_async_remote_copy(
            src_ref=band.at[it, 1, :, :, pl.ds(c * part, part), :],
            dst_ref=band.at[it, side, :, :, pl.ds(c * part, part), :],
            send_sem=h_send.at[it, c, side // 2], recv_sem=h_recv.at[it, c, side // 2],
            device_id={"energy": right if side == 0 else left}, device_id_type=MESH)

    def homeward(it, c, j):
        return pltpu.make_async_remote_copy(
            src_ref=mixed.at[it, peer(j), :, pl.ds(c * part, part), :],
            dst_ref=back.at[it, :, span(me, c), :],
            send_sem=b_send.at[it, c, j], recv_sem=b_recv.at[it, c, j],
            device_id={"momentum": peer(j)}, device_id_type=MESH)

    def mix(it, c):
        def step(n, carry):
            r = pl.ds(pl.multiple_of(c * part + n * PACK, PACK), PACK)

            def at(i, q):
                side, i = (0, i + energies) if i < 0 else (1, i) if i < energies else (2, i - energies)
                return band[it, side, i, q, r, :].astype(jnp.float32).reshape(2, PACK // 2, tile)

            for i in range(energies):
                pair = [[at(i - d, q) + at(i + d, q) for q in range(nk)] for d in range(1, OMAX + 1)]

                def one(k, inner):
                    total = None
                    for d in range(OMAX):
                        for q in range(nk):
                            term = weights[d, k, q][None] * pair[d][q]
                            total = term if total is None else total + term
                    mixed[it, k, i, r, :] = total.reshape(PACK, tile).astype(jnp.bfloat16)
                    return inner

                if nk <= 4:
                    for k in range(nk):
                        one(k, 0)
                else:
                    lax.fori_loop(0, nk, one, 0)
            return carry

        lax.fori_loop(0, part // PACK, step, 0)

    pl.semaphore_wait(barrier, nk - 1 + has_left.astype(jnp.int32) + has_right.astype(jnp.int32))
    loads[0].wait()
    source = start
    for it in range(ITERS):
        for i in range(energies):
            if it == 0:
                loads[1 + i].wait()
            onsite(it, i, source)
        for c in range(chunks):
            for j in range(1, nk):
                outward(it, c, j).start()
        mine = pltpu.make_async_copy(lesser.at[it, :, pl.ds(pl.multiple_of(me * rows, PACK), rows), :],
                                     band.at[it, 1, :, me], own_sem.at[it, chunks])
        mine.start()
        if it == ITERS - 1:
            store = pltpu.make_async_copy(lesser.at[it], lesser_out, out_sem.at[0])
            store.start()
        mine.wait()
        keeps = []
        for c in range(chunks + 1):
            if c < chunks:
                for j in range(1, nk):
                    outward(it, c, j).wait_recv()

                @pl.when(has_right)
                def _():
                    halo(it, c, 0).start()

                @pl.when(has_left)
                def _():
                    halo(it, c, 2).start()
            if c > 0:
                b = c - 1

                @pl.when(has_left)
                def _():
                    halo(it, b, 0).wait_recv()

                @pl.when(has_right)
                def _():
                    halo(it, b, 2).wait_recv()

                mix(it, b)
                for j in range(1, nk):
                    homeward(it, b, j).start()
                keep = pltpu.make_async_copy(mixed.at[it, me, :, pl.ds(b * part, part), :],
                                             back.at[it, :, span(me, b), :], own_sem.at[it, b])
                keep.start()
                keeps.append(keep)
        for c in range(chunks):
            keeps[c].wait()
            for j in range(1, nk):
                homeward(it, c, j).wait_recv()
        for i in range(energies):
            def add(n, carry):
                r = pl.ds(pl.multiple_of(n * tile, tile), tile)
                total = start[i, r, :].astype(jnp.float32) + back[it, i, r, :].astype(jnp.float32)
                sigma[it, i, r, :] = total.astype(jnp.bfloat16)
                return carry
            lax.fori_loop(0, 2 * tiles, add, 0)
        source = sigma.at[it]

    final = pltpu.make_async_copy(sigma.at[ITERS - 1], sigma_out, out_sem.at[1])
    final.start()
    for it in range(ITERS):
        for c in range(chunks):
            for j in range(1, nk):
                outward(it, c, j).wait_send()
                homeward(it, c, j).wait_send()

            @pl.when(has_right)
            def _():
                halo(it, c, 0).wait_send()

            @pl.when(has_left)
            def _():
                halo(it, c, 2).wait_send()
    store.wait()
    final.wait()


def body(ne, nk, green, contact, counts, offsets, pairs, table):
    energies, order = green.shape[0], green.shape[-1]
    tile = contact.shape[-1]
    height = contact.shape[2] * contact.shape[3] * tile
    rows = height // nk
    chunks = max(c for c in range(1, CHUNKS + 1) if rows % (c * PACK) == 0)
    blocks = green.reshape(energies, 2, order, order)
    flat = contact.reshape(energies, height, tile)
    half = jnp.bfloat16
    result = jax.ShapeDtypeStruct(flat.shape, half)
    dma = pltpu.SemaphoreType.DMA
    anywhere = pl.BlockSpec(memory_space=pl.ANY)
    scalars = pl.BlockSpec(memory_space=pltpu.SMEM)
    lesser, sigma = pl.pallas_call(
        functools.partial(born, ne, nk, chunks),
        out_shape=(result, result),
        in_specs=[anywhere] * 2 + [scalars] * 4,
        out_specs=(anywhere, anywhere),
        scratch_shapes=[
            pltpu.VMEM(blocks.shape, half),
            pltpu.VMEM(flat.shape, half),
            pltpu.VMEM((2, order, order), half),
            pltpu.VMEM((ITERS,) + flat.shape, half),
            pltpu.VMEM((ITERS, 3, energies, nk, rows, tile), half),
            pltpu.VMEM((ITERS, nk, energies, rows, tile), half),
            pltpu.VMEM((ITERS,) + flat.shape, half),
            pltpu.VMEM((ITERS,) + flat.shape, half),
            pltpu.VMEM((OMAX, nk, nk, 8, tile), jnp.float32),
            dma((energies + 1,)),
            dma((ITERS, chunks + 1)),
            dma((2,)),
            dma((ITERS, chunks, nk)),
            dma((ITERS, chunks, nk)),
            dma((ITERS, chunks, 2)),
            dma((ITERS, chunks, 2)),
            dma((ITERS, chunks, nk)),
            dma((ITERS, chunks, nk)),
        ],
        compiler_params=pltpu.CompilerParams(
            collective_id=0, has_side_effects=True, vmem_limit_bytes=40 * 2**20
        ),
    )(blocks, flat, counts, offsets, pairs, table)
    return lesser.reshape(contact.shape), sigma.reshape(contact.shape)


def solution(mesh):
    blocks = P("energy", "momentum", None, None, None)
    tiles = P("energy", "momentum", None, None, None, None)
    run = functools.partial(body, mesh.shape["energy"], mesh.shape["momentum"])
    return jax.shard_map(run, mesh=mesh, in_specs=(blocks, tiles, P("energy"), P(), P(), P()),
                         out_specs=(tiles, tiles), check_vma=False)
```

```python
import functools

import jax
import jax.numpy as jnp
from jax import lax
from jax.experimental import pallas as pl
from jax.experimental.pallas import tpu as pltpu
from jax.sharding import PartitionSpec as P

OMAX = 3
ITERS = 2
PACK = 16
CHUNKS = 3
MESH = pl.DeviceIdType.MESH


def born(ne, nk, chunks, green, contact, counts, offsets, pairs, table, lesser_out, sigma_out,
         g, start, product, lesser, band, mixed, back, sigma, weights,
         in_sem, own_sem, out_sem, a_send, a_recv, h_send, h_recv, b_send, b_recv):
    energies, order = g.shape[0], g.shape[-1]
    tile = start.shape[-1]
    tiles = order // tile
    rows = band.shape[4]
    part = rows // chunks
    modes = offsets.shape[0]
    e, me = lax.axis_index("energy"), lax.axis_index("momentum")
    has_left, has_right = e > 0, e < ne - 1
    left, right = jnp.maximum(e - 1, 0), jnp.minimum(e + 1, ne - 1)

    loads = []
    for i in range(energies):
        loads.append((pltpu.make_async_copy(contact.at[i], start.at[i], in_sem.at[0, i]),
                      pltpu.make_async_copy(green.at[i], g.at[i], in_sem.at[1, i])))
        for load in loads[i]:
            load.start()

    out_pieces = [(0, i, 1) for i in range(energies)] + [(c, 0, energies) for c in range(1, chunks)]
    home_pieces = [(c, 0, energies) for c in range(chunks - 1)]
    home_pieces += [(chunks - 1, i, 1) for i in range(energies)]

    def peer(j):
        return lax.rem(me + j, nk)

    barrier = pltpu.get_barrier_semaphore()
    for j in range(1, nk):
        pl.semaphore_signal(barrier, inc=1, device_id={"momentum": peer(j)}, device_id_type=MESH)

    @pl.when(has_left)
    def _():
        pl.semaphore_signal(barrier, inc=1, device_id={"energy": left}, device_id_type=MESH)

    @pl.when(has_right)
    def _():
        pl.semaphore_signal(barrier, inc=1, device_id={"energy": right}, device_id_type=MESH)

    def weigh(i, carry):
        k, q = i // nk, i % nk
        sums = [jnp.float32(0)] * OMAX
        for m in range(modes):
            value = table[m, pairs[m, k, q]]
            for d in range(OMAX):
                sums[d] = sums[d] + jnp.where(offsets[m] == d + 1, value, jnp.float32(0))
        for d in range(OMAX):
            weights[d, k, q] = jnp.full(weights.shape[3:], sums[d], jnp.float32)
        return carry

    def clear(side):
        for it in range(ITERS):
            for i in range(energies):
                def zero(q, carry):
                    band[it, side, i, q] = jnp.zeros(band.shape[4:], band.dtype)
                    return carry
                lax.fori_loop(0, nk, zero, 0)

    def prepare():
        lax.fori_loop(0, nk * nk, weigh, 0)

        @pl.when(e == 0)
        def _():
            clear(0)

        @pl.when(e == ne - 1)
        def _():
            clear(2)

    def onsite(it, i, source):
        for t in range(tiles):
            cols = slice(t * tile, (t + 1) * tile)
            s_real = source[i, t * tile:(t + 1) * tile, :]
            s_imag = source[i, (tiles + t) * tile:(tiles + t + 1) * tile, :]
            s = jnp.concatenate([jnp.concatenate([s_real, s_imag], 1),
                                 jnp.concatenate([-s_imag, s_real], 1)], 0)
            a = jnp.concatenate([g[i, 0, :, cols], g[i, 1, :, cols]], 1)
            p = jnp.dot(a, s, preferred_element_type=jnp.float32).astype(jnp.bfloat16)
            product[0, :, cols] = p[:, :tile]
            product[1, :, cols] = p[:, tile:]
        for t in range(tiles):
            r = slice(t * tile, (t + 1) * tile)
            p = jnp.concatenate([product[0, r, :], product[1, r, :]], 0)
            h = jnp.concatenate([g[i, 0, r, :], g[i, 1, r, :]], 0)
            o = lax.dot_general(p, h, (((1,), (1,)), ((), ())), preferred_element_type=jnp.float32)
            live = jnp.where(t < counts[i], jnp.float32(1), jnp.float32(0))
            real = (o[:tile, :tile] + o[tile:, tile:]) * live
            imag = (o[tile:, :tile] - o[:tile, tile:]) * live
            lesser[it, i, t * tile:(t + 1) * tile, :] = real.astype(jnp.bfloat16)
            lesser[it, i, (tiles + t) * tile:(tiles + t + 1) * tile, :] = imag.astype(jnp.bfloat16)

    def span(owner, c):
        return pl.ds(pl.multiple_of(owner * rows + c * part, PACK), part)

    def outward(it, n, j):
        c, i, w = out_pieces[n]
        return pltpu.make_async_remote_copy(
            src_ref=lesser.at[it, pl.ds(i, w), span(peer(j), c), :],
            dst_ref=band.at[it, 1, pl.ds(i, w), me, pl.ds(c * part, part), :],
            send_sem=a_send.at[it, n, j], recv_sem=a_recv.at[it, n, j],
            device_id={"momentum": peer(j)}, device_id_type=MESH)

    def halo(it, c, side):
        return pltpu.make_async_remote_copy(
            src_ref=band.at[it, 1, :, :, pl.ds(c * part, part), :],
            dst_ref=band.at[it, side, :, :, pl.ds(c * part, part), :],
            send_sem=h_send.at[it, c, side // 2], recv_sem=h_recv.at[it, c, side // 2],
            device_id={"energy": right if side == 0 else left}, device_id_type=MESH)

    def homeward(it, n, j):
        c, i, w = home_pieces[n]
        return pltpu.make_async_remote_copy(
            src_ref=mixed.at[it, peer(j), pl.ds(i, w), pl.ds(c * part, part), :],
            dst_ref=back.at[it, pl.ds(i, w), span(me, c), :],
            send_sem=b_send.at[it, n, j], recv_sem=b_recv.at[it, n, j],
            device_id={"momentum": peer(j)}, device_id_type=MESH)

    def keep(it, n):
        c, i, w = home_pieces[n]
        return pltpu.make_async_copy(mixed.at[it, me, pl.ds(i, w), pl.ds(c * part, part), :],
                                     back.at[it, pl.ds(i, w), span(me, c), :], own_sem.at[it, n])

    def mix(it, c, first, width):
        def step(n, carry):
            r = pl.ds(pl.multiple_of(c * part + n * PACK, PACK), PACK)

            def at(i, q):
                side, i = (0, i + energies) if i < 0 else (1, i) if i < energies else (2, i - energies)
                return band[it, side, i, q, r, :].astype(jnp.float32).reshape(2, PACK // 2, tile)

            for i in range(first, first + width):
                pair = [[at(i - d, q) + at(i + d, q) for q in range(nk)] for d in range(1, OMAX + 1)]

                def one(k, inner):
                    total = None
                    for d in range(OMAX):
                        for q in range(nk):
                            term = weights[d, k, q][None] * pair[d][q]
                            total = term if total is None else total + term
                    mixed[it, k, i, r, :] = total.reshape(PACK, tile).astype(jnp.bfloat16)
                    return inner

                if nk <= 4:
                    for k in range(nk):
                        one(k, 0)
                else:
                    lax.fori_loop(0, nk, one, 0)
            return carry

        lax.fori_loop(0, part // PACK, step, 0)

    def arrive(it, n):
        keep(it, n).wait()
        for j in range(1, nk):
            homeward(it, n, j).wait_recv()

    def renew(it, i):
        if i == 0:
            for n in range(chunks - 1):
                arrive(it, n)
        arrive(it, chunks - 1 + i)

        def add(n, carry):
            r = pl.ds(pl.multiple_of(n * tile, tile), tile)
            total = start[i, r, :].astype(jnp.float32) + back[it, i, r, :].astype(jnp.float32)
            sigma[it, i, r, :] = total.astype(jnp.bfloat16)
            return carry
        lax.fori_loop(0, 2 * tiles, add, 0)

    source = start
    for it in range(ITERS):
        for i in range(energies):
            if it == 0:
                for load in loads[i]:
                    load.wait()
            else:
                renew(it - 1, i)
            onsite(it, i, source)
            if it == 0 and i == 0:
                pl.semaphore_wait(
                    barrier, nk - 1 + has_left.astype(jnp.int32) + has_right.astype(jnp.int32))
            for j in range(1, nk):
                outward(it, i, j).start()
        for n in range(energies, len(out_pieces)):
            for j in range(1, nk):
                outward(it, n, j).start()
        mine = pltpu.make_async_copy(lesser.at[it, :, pl.ds(pl.multiple_of(me * rows, PACK), rows), :],
                                     band.at[it, 1, :, me], own_sem.at[it, len(home_pieces)])
        mine.start()
        if it == ITERS - 1:
            store = pltpu.make_async_copy(lesser.at[it], lesser_out, out_sem.at[energies])
            store.start()
        if it == 0:
            prepare()
        mine.wait()
        for c in range(chunks + 1):
            for n, (piece, _, _) in enumerate(out_pieces):
                if piece == c:
                    for j in range(1, nk):
                        outward(it, n, j).wait_recv()
            if c < chunks:
                @pl.when(has_right)
                def _():
                    halo(it, c, 0).start()

                @pl.when(has_left)
                def _():
                    halo(it, c, 2).start()
            if c > 0:
                @pl.when(has_left)
                def _():
                    halo(it, c - 1, 0).wait_recv()

                @pl.when(has_right)
                def _():
                    halo(it, c - 1, 2).wait_recv()

                for n, (piece, first, width) in enumerate(home_pieces):
                    if piece == c - 1:
                        mix(it, piece, first, width)
                        for j in range(1, nk):
                            homeward(it, n, j).start()
                        keep(it, n).start()
        source = sigma.at[it]

    last = ITERS - 1
    final = [pltpu.make_async_copy(sigma.at[last, i], sigma_out.at[i], out_sem.at[i])
             for i in range(energies)]
    for i in range(energies):
        renew(last, i)
        final[i].start()
    for it in range(ITERS):
        for n in range(len(out_pieces)):
            for j in range(1, nk):
                outward(it, n, j).wait_send()
                homeward(it, n, j).wait_send()
        for c in range(chunks):
            @pl.when(has_right)
            def _():
                halo(it, c, 0).wait_send()

            @pl.when(has_left)
            def _():
                halo(it, c, 2).wait_send()
    store.wait()
    for i in range(energies):
        final[i].wait()


def body(ne, nk, green, contact, counts, offsets, pairs, table):
    energies, order = green.shape[0], green.shape[-1]
    tile = contact.shape[-1]
    height = contact.shape[2] * contact.shape[3] * tile
    rows = height // nk
    chunks = max(c for c in range(1, CHUNKS + 1) if rows % (c * PACK) == 0)
    pieces = energies + chunks - 1
    blocks = green.reshape(energies, 2, order, order)
    flat = contact.reshape(energies, height, tile)
    half = jnp.bfloat16
    result = jax.ShapeDtypeStruct(flat.shape, half)
    dma = pltpu.SemaphoreType.DMA
    anywhere = pl.BlockSpec(memory_space=pl.ANY)
    scalars = pl.BlockSpec(memory_space=pltpu.SMEM)
    lesser, sigma = pl.pallas_call(
        functools.partial(born, ne, nk, chunks),
        out_shape=(result, result),
        in_specs=[anywhere] * 2 + [scalars] * 4,
        out_specs=(anywhere, anywhere),
        scratch_shapes=[
            pltpu.VMEM(blocks.shape, half),
            pltpu.VMEM(flat.shape, half),
            pltpu.VMEM((2, order, order), half),
            pltpu.VMEM((ITERS,) + flat.shape, half),
            pltpu.VMEM((ITERS, 3, energies, nk, rows, tile), half),
            pltpu.VMEM((ITERS, nk, energies, rows, tile), half),
            pltpu.VMEM((ITERS,) + flat.shape, half),
            pltpu.VMEM((ITERS,) + flat.shape, half),
            pltpu.VMEM((OMAX, nk, nk, 8, tile), jnp.float32),
            dma((2, energies)),
            dma((ITERS, pieces + 1)),
            dma((energies + 1,)),
            dma((ITERS, pieces, nk)),
            dma((ITERS, pieces, nk)),
            dma((ITERS, chunks, 2)),
            dma((ITERS, chunks, 2)),
            dma((ITERS, pieces, nk)),
            dma((ITERS, pieces, nk)),
        ],
        compiler_params=pltpu.CompilerParams(
            collective_id=0, has_side_effects=True, vmem_limit_bytes=60 * 2**20
        ),
    )(blocks, flat, counts, offsets, pairs, table)
    return lesser.reshape(contact.shape), sigma.reshape(contact.shape)


def solution(mesh):
    blocks = P("energy", "momentum", None, None, None)
    tiles = P("energy", "momentum", None, None, None, None)
    run = functools.partial(body, mesh.shape["energy"], mesh.shape["momentum"])
    return jax.shard_map(run, mesh=mesh, in_specs=(blocks, tiles, P("energy"), P(), P(), P()),
                         out_specs=(tiles, tiles), check_vma=False)
```

```python
import functools

import jax
import jax.numpy as jnp
from jax import lax
from jax.experimental import pallas as pl
from jax.experimental.pallas import tpu as pltpu
from jax.sharding import PartitionSpec as P

OMAX = 3
ITERS = 2
PACK = 16
CHUNKS = 4
MESH = pl.DeviceIdType.MESH


def born(ne, nk, chunks, green, contact, counts, offsets, pairs, table, lesser_out, sigma_out,
         g, start, product, lesser, band, mixed, back, sigma, weights,
         in_sem, own_sem, out_sem, a_send, a_recv, h_send, h_recv, b_send, b_recv):
    energies, order = g.shape[0], g.shape[-1]
    tile = start.shape[-1]
    tiles = order // tile
    rows = band.shape[4]
    part = rows // chunks
    modes = offsets.shape[0]
    e, me = lax.axis_index("energy"), lax.axis_index("momentum")
    has_left, has_right = e > 0, e < ne - 1
    left, right = jnp.maximum(e - 1, 0), jnp.minimum(e + 1, ne - 1)

    loads = []
    for i in range(energies):
        loads.append((pltpu.make_async_copy(contact.at[i], start.at[i], in_sem.at[0, i]),
                      pltpu.make_async_copy(green.at[i], g.at[i], in_sem.at[1, i])))
        for load in loads[i]:
            load.start()

    out_pieces = [(0, i, 1) for i in range(energies)] + [(c, 0, energies) for c in range(1, chunks)]
    home_pieces = [(c, 0, energies) for c in range(chunks - 1)]
    home_pieces += [(chunks - 1, i, 1) for i in range(energies)]

    def peer(j):
        return lax.rem(me + j, nk)

    barrier = pltpu.get_barrier_semaphore()
    for j in range(1, nk):
        pl.semaphore_signal(barrier, inc=1, device_id={"momentum": peer(j)}, device_id_type=MESH)

    @pl.when(has_left)
    def _():
        pl.semaphore_signal(barrier, inc=1, device_id={"energy": left}, device_id_type=MESH)

    @pl.when(has_right)
    def _():
        pl.semaphore_signal(barrier, inc=1, device_id={"energy": right}, device_id_type=MESH)

    def weigh(i, carry):
        k, q = i // nk, i % nk
        sums = [jnp.float32(0)] * OMAX
        for m in range(modes):
            value = table[m, pairs[m, k, q]]
            for d in range(OMAX):
                sums[d] = sums[d] + jnp.where(offsets[m] == d + 1, value, jnp.float32(0))
        for d in range(OMAX):
            weights[d, k, q] = jnp.full(weights.shape[3:], sums[d], jnp.float32)
        return carry

    def clear(side):
        for it in range(ITERS):
            for i in range(energies):
                def zero(q, carry):
                    band[it, side, i, q] = jnp.zeros(band.shape[4:], band.dtype)
                    return carry
                lax.fori_loop(0, nk, zero, 0)

    def prepare():
        lax.fori_loop(0, nk * nk, weigh, 0)

        @pl.when(e == 0)
        def _():
            clear(0)

        @pl.when(e == ne - 1)
        def _():
            clear(2)

    def onsite(it, i, source):
        for t in range(tiles):
            cols = slice(t * tile, (t + 1) * tile)
            s_real = source[i, t * tile:(t + 1) * tile, :]
            s_imag = source[i, (tiles + t) * tile:(tiles + t + 1) * tile, :]
            s = jnp.concatenate([jnp.concatenate([s_real, s_imag], 1),
                                 jnp.concatenate([-s_imag, s_real], 1)], 0)
            a = jnp.concatenate([g[i, 0, :, cols], g[i, 1, :, cols]], 1)
            p = jnp.dot(a, s, preferred_element_type=jnp.float32).astype(jnp.bfloat16)
            product[0, :, cols] = p[:, :tile]
            product[1, :, cols] = p[:, tile:]
        for t in range(tiles):
            r = slice(t * tile, (t + 1) * tile)
            p = jnp.concatenate([product[0, r, :], product[1, r, :]], 0)
            h = jnp.concatenate([g[i, 0, r, :], g[i, 1, r, :]], 0)
            o = lax.dot_general(p, h, (((1,), (1,)), ((), ())), preferred_element_type=jnp.float32)
            live = jnp.where(t < counts[i], jnp.float32(1), jnp.float32(0))
            real = (o[:tile, :tile] + o[tile:, tile:]) * live
            imag = (o[tile:, :tile] - o[:tile, tile:]) * live
            lesser[it, i, t * tile:(t + 1) * tile, :] = real.astype(jnp.bfloat16)
            lesser[it, i, (tiles + t) * tile:(tiles + t + 1) * tile, :] = imag.astype(jnp.bfloat16)

    def span(owner, c):
        return pl.ds(pl.multiple_of(owner * rows + c * part, PACK), part)

    def outward(it, n, j):
        c, i, w = out_pieces[n]
        return pltpu.make_async_remote_copy(
            src_ref=lesser.at[it, pl.ds(i, w), span(peer(j), c), :],
            dst_ref=band.at[it, 1, pl.ds(i, w), me, pl.ds(c * part, part), :],
            send_sem=a_send.at[it, n, j], recv_sem=a_recv.at[it, n, j],
            device_id={"momentum": peer(j)}, device_id_type=MESH)

    def halo(it, c, side):
        return pltpu.make_async_remote_copy(
            src_ref=band.at[it, 1, :, :, pl.ds(c * part, part), :],
            dst_ref=band.at[it, side, :, :, pl.ds(c * part, part), :],
            send_sem=h_send.at[it, c, side // 2], recv_sem=h_recv.at[it, c, side // 2],
            device_id={"energy": right if side == 0 else left}, device_id_type=MESH)

    def homeward(it, n, j):
        c, i, w = home_pieces[n]
        return pltpu.make_async_remote_copy(
            src_ref=mixed.at[it, peer(j), pl.ds(i, w), pl.ds(c * part, part), :],
            dst_ref=back.at[it, pl.ds(i, w), span(me, c), :],
            send_sem=b_send.at[it, n, j], recv_sem=b_recv.at[it, n, j],
            device_id={"momentum": peer(j)}, device_id_type=MESH)

    def keep(it, n):
        c, i, w = home_pieces[n]
        return pltpu.make_async_copy(mixed.at[it, me, pl.ds(i, w), pl.ds(c * part, part), :],
                                     back.at[it, pl.ds(i, w), span(me, c), :], own_sem.at[it, n])

    def mix(it, c, first, width):
        def step(n, carry):
            r = pl.ds(pl.multiple_of(c * part + n * PACK, PACK), PACK)

            def at(i, q):
                side, i = (0, i + energies) if i < 0 else (1, i) if i < energies else (2, i - energies)
                return band[it, side, i, q, r, :].astype(jnp.float32).reshape(2, PACK // 2, tile)

            for i in range(first, first + width):
                pair = [[at(i - d, q) + at(i + d, q) for q in range(nk)] for d in range(1, OMAX + 1)]

                def one(k, inner):
                    total = None
                    for d in range(OMAX):
                        for q in range(nk):
                            term = weights[d, k, q][None] * pair[d][q]
                            total = term if total is None else total + term
                    mixed[it, k, i, r, :] = total.reshape(PACK, tile).astype(jnp.bfloat16)
                    return inner

                if nk <= 4:
                    for k in range(nk):
                        one(k, 0)
                else:
                    lax.fori_loop(0, nk, one, 0)
            return carry

        lax.fori_loop(0, part // PACK, step, 0)

    def arrive(it, n):
        keep(it, n).wait()
        for j in range(1, nk):
            homeward(it, n, j).wait_recv()

    def renew(it, i, result):
        if i == 0:
            for n in range(chunks - 1):
                arrive(it, n)
        arrive(it, chunks - 1 + i)

        def add(n, carry):
            r = pl.ds(pl.multiple_of(n * tile, tile), tile)
            total = start[i, r, :].astype(jnp.float32) + back[it, i, r, :].astype(jnp.float32)
            result[i, r, :] = total.astype(jnp.bfloat16)
            return carry
        lax.fori_loop(0, 2 * tiles, add, 0)

    source = start
    for it in range(ITERS):
        for i in range(energies):
            if it == 0:
                for load in loads[i]:
                    load.wait()
            else:
                renew(it - 1, i, source)
            onsite(it, i, source)
            if it == 0 and i == 0:
                pl.semaphore_wait(
                    barrier, nk - 1 + has_left.astype(jnp.int32) + has_right.astype(jnp.int32))
            for j in range(1, nk):
                outward(it, i, j).start()
        for n in range(energies, len(out_pieces)):
            for j in range(1, nk):
                outward(it, n, j).start()
        mine = pltpu.make_async_copy(lesser.at[it, :, pl.ds(pl.multiple_of(me * rows, PACK), rows), :],
                                     band.at[it, 1, :, me], own_sem.at[it, len(home_pieces)])
        mine.start()
        if it == ITERS - 1:
            store = pltpu.make_async_copy(lesser.at[it], lesser_out, out_sem.at[0])
            store.start()
        if it == 0:
            prepare()
        mine.wait()
        for c in range(chunks + 1):
            for n, (piece, _, _) in enumerate(out_pieces):
                if piece == c:
                    for j in range(1, nk):
                        outward(it, n, j).wait_recv()
            if c < chunks:
                @pl.when(has_right)
                def _():
                    halo(it, c, 0).start()

                @pl.when(has_left)
                def _():
                    halo(it, c, 2).start()
            if c > 0:
                @pl.when(has_left)
                def _():
                    halo(it, c - 1, 0).wait_recv()

                @pl.when(has_right)
                def _():
                    halo(it, c - 1, 2).wait_recv()

                for n, (piece, first, width) in enumerate(home_pieces):
                    if piece == c - 1:
                        mix(it, piece, first, width)
                        for j in range(1, nk):
                            homeward(it, n, j).start()
                        keep(it, n).start()
        source = sigma.at[it] if it < ITERS - 1 else sigma_out

    for i in range(energies):
        renew(ITERS - 1, i, source)
    for it in range(ITERS):
        for n in range(len(out_pieces)):
            for j in range(1, nk):
                outward(it, n, j).wait_send()
                homeward(it, n, j).wait_send()
        for c in range(chunks):
            @pl.when(has_right)
            def _():
                halo(it, c, 0).wait_send()

            @pl.when(has_left)
            def _():
                halo(it, c, 2).wait_send()
    store.wait()


def write(*refs):
    count = (len(refs) - 1) // 2
    copies = [pltpu.make_async_copy(refs[i], refs[count + i], refs[-1].at[i]) for i in range(count)]
    for copy in copies:
        copy.start()
    for copy in copies:
        copy.wait()


def body(ne, nk, green, contact, counts, offsets, pairs, table):
    energies, order = green.shape[0], green.shape[-1]
    tile = contact.shape[-1]
    height = contact.shape[2] * contact.shape[3] * tile
    rows = height // nk
    chunks = max(c for c in range(1, CHUNKS + 1) if rows % (c * PACK) == 0)
    pieces = energies + chunks - 1
    blocks = green.reshape(energies, 2, order, order)
    flat = contact.reshape(energies, height, tile)
    half = jnp.bfloat16
    result = jax.ShapeDtypeStruct(flat.shape, half)
    dma = pltpu.SemaphoreType.DMA
    anywhere = pl.BlockSpec(memory_space=pl.ANY)
    far = pl.BlockSpec(memory_space=pltpu.HBM)
    near = pl.BlockSpec(memory_space=pltpu.VMEM)
    scalars = pl.BlockSpec(memory_space=pltpu.SMEM)
    results = pl.pallas_call(
        functools.partial(born, ne, nk, chunks),
        out_shape=(pltpu.VMEM(flat.shape, half),) * 2,
        in_specs=[far] * 2 + [scalars] * 4,
        out_specs=(near, near),
        scratch_shapes=[
            pltpu.VMEM(blocks.shape, half),
            pltpu.VMEM(flat.shape, half),
            pltpu.VMEM((2, order, order), half),
            pltpu.VMEM((ITERS,) + flat.shape, half),
            pltpu.VMEM((ITERS, 3, energies, nk, rows, tile), half),
            pltpu.VMEM((ITERS, nk, energies, rows, tile), half),
            pltpu.VMEM((ITERS,) + flat.shape, half),
            pltpu.VMEM((ITERS - 1,) + flat.shape, half),
            pltpu.VMEM((OMAX, nk, nk, 8, tile), jnp.float32),
            dma((2, energies)),
            dma((ITERS, pieces + 1)),
            dma((1,)),
            dma((ITERS, pieces, nk)),
            dma((ITERS, pieces, nk)),
            dma((ITERS, chunks, 2)),
            dma((ITERS, chunks, 2)),
            dma((ITERS, pieces, nk)),
            dma((ITERS, pieces, nk)),
        ],
        compiler_params=pltpu.CompilerParams(
            collective_id=0, has_side_effects=True, vmem_limit_bytes=56 * 2**20
        ),
    )(blocks, flat, counts, offsets, pairs, table)
    lesser, sigma = pl.pallas_call(
        write,
        out_shape=(result, result),
        in_specs=[anywhere] * 2,
        out_specs=(far, far),
        scratch_shapes=[dma((2,))],
    )(*results)
    return lesser.reshape(contact.shape), sigma.reshape(contact.shape)


def solution(mesh):
    blocks = P("energy", "momentum", None, None, None)
    tiles = P("energy", "momentum", None, None, None, None)
    run = functools.partial(body, mesh.shape["energy"], mesh.shape["momentum"])
    return jax.shard_map(run, mesh=mesh, in_specs=(blocks, tiles, P("energy"), P(), P(), P()),
                         out_specs=(tiles, tiles), check_vma=False)
```

```python
import functools

import jax
import jax.numpy as jnp
from jax import lax
from jax.experimental import pallas as pl
from jax.experimental.pallas import tpu as pltpu
from jax.sharding import PartitionSpec as P

OMAX = 3
ITERS = 2
PACK = 16
MESH = pl.DeviceIdType.MESH


def born(ne, nk, green, contact, counts, offsets, pairs, table, lesser_out, sigma_out,
         g, start, product, lesser, band, mixed, back, sigma, weights,
         in_sem, own_sem, a_send, a_recv, h_send, h_recv, b_send, b_recv):
    energies, order = g.shape[0], g.shape[-1]
    tile = start.shape[-1]
    tiles = order // tile
    rows = band.shape[4]
    chunks = tiles
    part = rows // chunks
    modes = offsets.shape[0]
    e, me = lax.axis_index("energy"), lax.axis_index("momentum")
    has_left, has_right = e > 0, e < ne - 1
    left, right = jnp.maximum(e - 1, 0), jnp.minimum(e + 1, ne - 1)

    loads = []
    for i in range(energies):
        loads.append((pltpu.make_async_copy(contact.at[i], start.at[i], in_sem.at[0, i]),
                      pltpu.make_async_copy(green.at[i], g.at[i], in_sem.at[1, i])))
        for load in loads[i]:
            load.start()

    out_pieces = [(0, i, 1) for i in range(energies)] + [(c, 0, energies) for c in range(1, chunks)]
    home_pieces = [(c, 0, energies) for c in range(chunks - 1)]
    home_pieces += [(chunks - 1, i, 1) for i in range(energies)]

    def peer(j):
        return lax.rem(me + j, nk)

    barrier = pltpu.get_barrier_semaphore()
    for j in range(1, nk):
        pl.semaphore_signal(barrier, inc=1, device_id={"momentum": peer(j)}, device_id_type=MESH)

    @pl.when(has_left)
    def _():
        pl.semaphore_signal(barrier, inc=1, device_id={"energy": left}, device_id_type=MESH)

    @pl.when(has_right)
    def _():
        pl.semaphore_signal(barrier, inc=1, device_id={"energy": right}, device_id_type=MESH)

    def weigh(i, carry):
        k, q = i // nk, i % nk
        sums = [jnp.float32(0)] * OMAX
        for m in range(modes):
            value = table[m, pairs[m, k, q]]
            for d in range(OMAX):
                sums[d] = sums[d] + jnp.where(offsets[m] == d + 1, value, jnp.float32(0))
        for d in range(OMAX):
            weights[d, k, q] = jnp.full(weights.shape[3:], sums[d], jnp.float32)
        return carry

    def clear(side):
        for it in range(ITERS):
            for i in range(energies):
                def zero(q, carry):
                    band[it, side, i, q] = jnp.zeros(band.shape[4:], band.dtype)
                    return carry
                lax.fori_loop(0, nk, zero, 0)

    def prepare():
        lax.fori_loop(0, nk * nk, weigh, 0)

        @pl.when(e == 0)
        def _():
            clear(0)

        @pl.when(e == ne - 1)
        def _():
            clear(2)

    def project(i, t, source):
        cols = slice(t * tile, (t + 1) * tile)
        s_real, s_imag = source[i, 0, t], source[i, 1, t]
        s = jnp.concatenate([jnp.concatenate([s_real, s_imag], 1),
                             jnp.concatenate([-s_imag, s_real], 1)], 0)
        a = jnp.concatenate([g[i, 0, :, cols], g[i, 1, :, cols]], 1)
        p = jnp.dot(a, s, preferred_element_type=jnp.float32).astype(jnp.bfloat16)
        product[i, 0, :, cols] = p[:, :tile]
        product[i, 1, :, cols] = p[:, tile:]

    def onsite(it, i, t):
        r = slice(t * tile, (t + 1) * tile)
        p = jnp.concatenate([product[i, 0, r, :], product[i, 1, r, :]], 0)
        h = jnp.concatenate([g[i, 0, r, :], g[i, 1, r, :]], 0)
        o = lax.dot_general(p, h, (((1,), (1,)), ((), ())), preferred_element_type=jnp.float32)
        live = jnp.where(t < counts[i], jnp.float32(1), jnp.float32(0))
        real = ((o[:tile, :tile] + o[tile:, tile:]) * live).astype(jnp.bfloat16)
        imag = ((o[tile:, :tile] - o[:tile, tile:]) * live).astype(jnp.bfloat16)
        lesser[it, i, 2 * t * tile:(2 * t + 1) * tile, :] = real
        lesser[it, i, (2 * t + 1) * tile:(2 * t + 2) * tile, :] = imag
        if it == ITERS - 1:
            lesser_out[i, 0, t] = real
            lesser_out[i, 1, t] = imag

    def span(owner, c):
        return pl.ds(pl.multiple_of(c * 2 * tile + owner * part, PACK), part)

    def outward(it, n, j):
        c, i, w = out_pieces[n]
        return pltpu.make_async_remote_copy(
            src_ref=lesser.at[it, pl.ds(i, w), span(peer(j), c), :],
            dst_ref=band.at[it, 1, pl.ds(i, w), me, pl.ds(c * part, part), :],
            send_sem=a_send.at[it, n, j], recv_sem=a_recv.at[it, n, j],
            device_id={"momentum": peer(j)}, device_id_type=MESH)

    def mine(it, n):
        c, i, w = out_pieces[n]
        return pltpu.make_async_copy(lesser.at[it, pl.ds(i, w), span(me, c), :],
                                     band.at[it, 1, pl.ds(i, w), me, pl.ds(c * part, part), :],
                                     own_sem.at[it, 0, n])

    def send(it, n):
        for j in range(1, nk):
            outward(it, n, j).start()
        mine(it, n).start()

    def halo(it, c, side):
        return pltpu.make_async_remote_copy(
            src_ref=band.at[it, 1, :, :, pl.ds(c * part, part), :],
            dst_ref=band.at[it, side, :, :, pl.ds(c * part, part), :],
            send_sem=h_send.at[it, c, side // 2], recv_sem=h_recv.at[it, c, side // 2],
            device_id={"energy": right if side == 0 else left}, device_id_type=MESH)

    def homeward(it, n, j):
        c, i, w = home_pieces[n]
        return pltpu.make_async_remote_copy(
            src_ref=mixed.at[it, peer(j), pl.ds(i, w), pl.ds(c * part, part), :],
            dst_ref=back.at[it, pl.ds(i, w), span(me, c), :],
            send_sem=b_send.at[it, n, j], recv_sem=b_recv.at[it, n, j],
            device_id={"momentum": peer(j)}, device_id_type=MESH)

    def keep(it, n):
        c, i, w = home_pieces[n]
        return pltpu.make_async_copy(mixed.at[it, me, pl.ds(i, w), pl.ds(c * part, part), :],
                                     back.at[it, pl.ds(i, w), span(me, c), :], own_sem.at[it, 1, n])

    def mix(it, c, first, width):
        def step(n, carry):
            r = pl.ds(pl.multiple_of(c * part + n * PACK, PACK), PACK)

            def at(i, q):
                side, i = (0, i + energies) if i < 0 else (1, i) if i < energies else (2, i - energies)
                return band[it, side, i, q, r, :].astype(jnp.float32).reshape(2, PACK // 2, tile)

            for i in range(first, first + width):
                pair = [[at(i - d, q) + at(i + d, q) for q in range(nk)] for d in range(1, OMAX + 1)]

                def one(k, inner):
                    total = None
                    for d in range(OMAX):
                        for q in range(nk):
                            term = weights[d, k, q][None] * pair[d][q]
                            total = term if total is None else total + term
                    mixed[it, k, i, r, :] = total.reshape(PACK, tile).astype(jnp.bfloat16)
                    return inner

                if nk <= 4:
                    for k in range(nk):
                        one(k, 0)
                else:
                    lax.fori_loop(0, nk, one, 0)
            return carry

        lax.fori_loop(0, part // PACK, step, 0)

    def arrive(it, n):
        keep(it, n).wait()
        for j in range(1, nk):
            homeward(it, n, j).wait_recv()

    def renew(it, i, t, result):
        for x in range(2):
            r = slice((2 * t + x) * tile, (2 * t + x + 1) * tile)
            total = start[i, x, t].astype(jnp.float32) + back[it, i, r, :].astype(jnp.float32)
            result[i, x, t] = total.astype(jnp.bfloat16)

    for it in range(ITERS):
        if it == 0:
            for i in range(energies):
                for load in loads[i]:
                    load.wait()
                for t in range(tiles):
                    project(i, t, start)
                onsite(it, i, 0)
                if i == 0:
                    pl.semaphore_wait(
                        barrier, nk - 1 + has_left.astype(jnp.int32) + has_right.astype(jnp.int32))
                send(it, i)
        else:
            for n, (t, first, width) in enumerate(home_pieces):
                arrive(it - 1, n)
                for i in range(first, first + width):
                    renew(it - 1, i, t, sigma.at[it - 1])
                    project(i, t, sigma.at[it - 1])
            for i in range(energies):
                onsite(it, i, 0)
                send(it, i)
        for n in range(energies, len(out_pieces)):
            t = out_pieces[n][0]
            for i in range(energies):
                onsite(it, i, t)
            send(it, n)
        if it == 0:
            prepare()
        for c in range(chunks + 1):
            for n, (piece, _, _) in enumerate(out_pieces):
                if piece == c:
                    mine(it, n).wait()
                    for j in range(1, nk):
                        outward(it, n, j).wait_recv()
            if c < chunks:
                @pl.when(has_right)
                def _():
                    halo(it, c, 0).start()

                @pl.when(has_left)
                def _():
                    halo(it, c, 2).start()
            if c > 0:
                @pl.when(has_left)
                def _():
                    halo(it, c - 1, 0).wait_recv()

                @pl.when(has_right)
                def _():
                    halo(it, c - 1, 2).wait_recv()

                for n, (piece, first, width) in enumerate(home_pieces):
                    if piece == c - 1:
                        mix(it, piece, first, width)
                        for j in range(1, nk):
                            homeward(it, n, j).start()
                        keep(it, n).start()

    for n, (t, first, width) in enumerate(home_pieces):
        arrive(ITERS - 1, n)
        for i in range(first, first + width):
            renew(ITERS - 1, i, t, sigma_out)
    for it in range(ITERS):
        for n in range(len(out_pieces)):
            for j in range(1, nk):
                outward(it, n, j).wait_send()
                homeward(it, n, j).wait_send()
        for c in range(chunks):
            @pl.when(has_right)
            def _():
                halo(it, c, 0).wait_send()

            @pl.when(has_left)
            def _():
                halo(it, c, 2).wait_send()


def write(*refs):
    count = (len(refs) - 1) // 2
    copies = [pltpu.make_async_copy(refs[i], refs[count + i], refs[-1].at[i]) for i in range(count)]
    for copy in copies:
        copy.start()
    for copy in copies:
        copy.wait()


def body(ne, nk, green, contact, counts, offsets, pairs, table):
    energies, order = green.shape[0], green.shape[-1]
    tile = contact.shape[-1]
    height = contact.shape[2] * contact.shape[3] * tile
    rows = height // nk
    chunks = contact.shape[3]
    pieces = energies + chunks - 1
    blocks = green.reshape(energies, 2, order, order)
    parted = contact.reshape((energies,) + contact.shape[2:])
    flat = jax.ShapeDtypeStruct((energies, height, tile), contact.dtype)
    half = jnp.bfloat16
    result = jax.ShapeDtypeStruct(parted.shape, half)
    dma = pltpu.SemaphoreType.DMA
    anywhere = pl.BlockSpec(memory_space=pl.ANY)
    far = pl.BlockSpec(memory_space=pltpu.HBM)
    near = pl.BlockSpec(memory_space=pltpu.VMEM)
    scalars = pl.BlockSpec(memory_space=pltpu.SMEM)
    results = pl.pallas_call(
        functools.partial(born, ne, nk),
        out_shape=(pltpu.VMEM(parted.shape, half),) * 2,
        in_specs=[far] * 2 + [scalars] * 4,
        out_specs=(near, near),
        scratch_shapes=[
            pltpu.VMEM(blocks.shape, half),
            pltpu.VMEM(parted.shape, half),
            pltpu.VMEM(blocks.shape, half),
            pltpu.VMEM((ITERS,) + flat.shape, half),
            pltpu.VMEM((ITERS, 3, energies, nk, rows, tile), half),
            pltpu.VMEM((ITERS, nk, energies, rows, tile), half),
            pltpu.VMEM((ITERS,) + flat.shape, half),
            pltpu.VMEM((ITERS - 1,) + parted.shape, half),
            pltpu.VMEM((OMAX, nk, nk, 8, tile), jnp.float32),
            dma((2, energies)),
            dma((ITERS, 2, pieces)),
            dma((ITERS, pieces, nk)),
            dma((ITERS, pieces, nk)),
            dma((ITERS, chunks, 2)),
            dma((ITERS, chunks, 2)),
            dma((ITERS, pieces, nk)),
            dma((ITERS, pieces, nk)),
        ],
        compiler_params=pltpu.CompilerParams(
            collective_id=0, has_side_effects=True, vmem_limit_bytes=56 * 2**20
        ),
    )(blocks, parted, counts, offsets, pairs, table)
    lesser, sigma = pl.pallas_call(
        write,
        out_shape=(result, result),
        in_specs=[near] * 2,
        out_specs=(anywhere, anywhere),
        scratch_shapes=[dma((2,))],
        compiler_params=pltpu.CompilerParams(vmem_limit_bytes=4 * 2**20),
    )(*results)
    return lesser.reshape(contact.shape), sigma.reshape(contact.shape)


def solution(mesh):
    blocks = P("energy", "momentum", None, None, None)
    tiles = P("energy", "momentum", None, None, None, None)
    run = functools.partial(body, mesh.shape["energy"], mesh.shape["momentum"])
    return jax.shard_map(run, mesh=mesh, in_specs=(blocks, tiles, P("energy"), P(), P(), P()),
                         out_specs=(tiles, tiles), check_vma=False)
```

```python
import functools
import math

import jax
import jax.numpy as jnp
from jax import lax
from jax.experimental import pallas as pl
from jax.experimental.pallas import tpu as pltpu
from jax.sharding import PartitionSpec as P

OMAX = 3
ITERS = 2
PACK = 16
MESH = pl.DeviceIdType.MESH


def born(ne, nk, green, contact, counts, offsets, pairs, table, lesser_out, sigma_out,
         g, start, product, lesser, band, mixed, back, sigma, weights,
         in_sem, own_sem, a_send, a_recv, h_send, h_recv, b_send, b_recv):
    energies, order = g.shape[0], g.shape[-1]
    tile = start.shape[-1]
    tiles = order // tile
    rows = band.shape[4]
    chunks = tiles
    part = rows // chunks
    modes = offsets.shape[0]
    e, me = lax.axis_index("energy"), lax.axis_index("momentum")
    odd = lax.rem(e, 2)
    near, far = e + 1 - 2 * odd, e - 1 + 2 * odd
    has_near, has_far = near < ne, (far >= 0) & (far < ne)

    loads = []
    for i in range(energies):
        loads.append((pltpu.make_async_copy(contact.at[i], start.at[i], in_sem.at[0, i]),
                      pltpu.make_async_copy(green.at[i], g.at[i], in_sem.at[1, i])))
        for load in loads[i]:
            load.start()

    out_pieces = [(0, i, 1) for i in range(energies)] + [(c, 0, energies) for c in range(1, chunks)]
    home_pieces = [(c, 0, energies) for c in range(chunks - 1)]
    home_pieces += [(chunks - 1, i, 1) for i in range(energies)]

    side = math.isqrt(nk)

    def peer(j):
        if side * side != nk:
            return lax.rem(me + j, nk)
        high, low = j // side, j % side
        high, low = high + odd * (low - high), low + odd * (high - low)
        return lax.rem(me // side + high, side) * side + lax.rem(me % side + low, side)

    barrier = pltpu.get_barrier_semaphore()
    for j in range(1, nk):
        pl.semaphore_signal(barrier, inc=1, device_id={"momentum": peer(j)}, device_id_type=MESH)

    @pl.when(has_near)
    def _():
        pl.semaphore_signal(barrier, inc=1, device_id={"energy": near}, device_id_type=MESH)

    @pl.when(has_far)
    def _():
        pl.semaphore_signal(barrier, inc=1, device_id={"energy": far}, device_id_type=MESH)

    def weigh(i, carry):
        k, q = i // nk, i % nk
        sums = [jnp.float32(0)] * OMAX
        for m in range(modes):
            value = table[m, pairs[m, k, q]]
            for d in range(OMAX):
                sums[d] = sums[d] + jnp.where(offsets[m] == d + 1, value, jnp.float32(0))
        for d in range(OMAX):
            weights[d, k, q] = jnp.full(weights.shape[3:], sums[d], jnp.float32)
        return carry

    def clear(side):
        for it in range(ITERS):
            for i in range(energies):
                def zero(q, carry):
                    band[it, side, i, q] = jnp.zeros(band.shape[4:], band.dtype)
                    return carry
                lax.fori_loop(0, nk, zero, 0)

    def prepare():
        lax.fori_loop(0, nk * nk, weigh, 0)

        @pl.when(e == 0)
        def _():
            clear(0)

        @pl.when(e == ne - 1)
        def _():
            clear(2)

    def project(i, t, source):
        cols = slice(t * tile, (t + 1) * tile)
        s_real, s_imag = source[i, 0, t], source[i, 1, t]
        s = jnp.concatenate([jnp.concatenate([s_real, s_imag], 1),
                             jnp.concatenate([-s_imag, s_real], 1)], 0)
        a = jnp.concatenate([g[i, 0, :, cols], g[i, 1, :, cols]], 1)
        p = jnp.dot(a, s, preferred_element_type=jnp.float32).astype(jnp.bfloat16)
        product[i, 0, :, cols] = p[:, :tile]
        product[i, 1, :, cols] = p[:, tile:]

    def onsite(it, i, t):
        r = slice(t * tile, (t + 1) * tile)
        p = jnp.concatenate([product[i, 0, r, :], product[i, 1, r, :]], 0)
        h = jnp.concatenate([g[i, 0, r, :], g[i, 1, r, :]], 0)
        o = lax.dot_general(p, h, (((1,), (1,)), ((), ())), preferred_element_type=jnp.float32)
        live = jnp.where(t < counts[i], jnp.float32(1), jnp.float32(0))
        real = ((o[:tile, :tile] + o[tile:, tile:]) * live).astype(jnp.bfloat16)
        imag = ((o[tile:, :tile] - o[:tile, tile:]) * live).astype(jnp.bfloat16)
        lesser[it, i, 2 * t * tile:(2 * t + 1) * tile, :] = real
        lesser[it, i, (2 * t + 1) * tile:(2 * t + 2) * tile, :] = imag
        if it == ITERS - 1:
            lesser_out[i, 0, t] = real
            lesser_out[i, 1, t] = imag

    def span(owner, c):
        return pl.ds(pl.multiple_of(c * 2 * tile + owner * part, PACK), part)

    def outward(it, n, j):
        c, i, w = out_pieces[n]
        return pltpu.make_async_remote_copy(
            src_ref=lesser.at[it, pl.ds(i, w), span(peer(j), c), :],
            dst_ref=band.at[it, 1, pl.ds(i, w), me, pl.ds(c * part, part), :],
            send_sem=a_send.at[it, n, j], recv_sem=a_recv.at[it, n, j],
            device_id={"momentum": peer(j)}, device_id_type=MESH)

    def mine(it, n):
        c, i, w = out_pieces[n]
        return pltpu.make_async_copy(lesser.at[it, pl.ds(i, w), span(me, c), :],
                                     band.at[it, 1, pl.ds(i, w), me, pl.ds(c * part, part), :],
                                     own_sem.at[it, 0, n])

    def send(it, n):
        for j in range(1, nk):
            outward(it, n, j).start()
        mine(it, n).start(priority=1)

    def halo(it, c, step):
        to = (near, far)[step]
        return pltpu.make_async_remote_copy(
            src_ref=band.at[it, 1, :, :, pl.ds(c * part, part), :],
            dst_ref=band.at[it, 1 + e - to, :, :, pl.ds(c * part, part), :],
            send_sem=h_send.at[it, c, step], recv_sem=h_recv.at[it, c, step],
            device_id={"energy": to}, device_id_type=MESH)

    def homeward(it, n, j):
        c, i, w = home_pieces[n]
        return pltpu.make_async_remote_copy(
            src_ref=mixed.at[it, peer(j), pl.ds(i, w), pl.ds(c * part, part), :],
            dst_ref=back.at[it, pl.ds(i, w), span(me, c), :],
            send_sem=b_send.at[it, n, j], recv_sem=b_recv.at[it, n, j],
            device_id={"momentum": peer(j)}, device_id_type=MESH)

    def keep(it, n):
        c, i, w = home_pieces[n]
        return pltpu.make_async_copy(mixed.at[it, me, pl.ds(i, w), pl.ds(c * part, part), :],
                                     back.at[it, pl.ds(i, w), span(me, c), :], own_sem.at[it, 1, n])

    def mix(it, c, first, width):
        def step(n, carry):
            r = pl.ds(pl.multiple_of(c * part + n * PACK, PACK), PACK)

            def at(i, q):
                side, i = (0, i + energies) if i < 0 else (1, i) if i < energies else (2, i - energies)
                return band[it, side, i, q, r, :].astype(jnp.float32).reshape(2, PACK // 2, tile)

            for i in range(first, first + width):
                pair = [[at(i - d, q) + at(i + d, q) for q in range(nk)] for d in range(1, OMAX + 1)]

                def one(k, inner):
                    total = None
                    for d in range(OMAX):
                        for q in range(nk):
                            term = weights[d, k, q][None] * pair[d][q]
                            total = term if total is None else total + term
                    mixed[it, k, i, r, :] = total.reshape(PACK, tile).astype(jnp.bfloat16)
                    return inner

                if nk <= 4:
                    for k in range(nk):
                        one(k, 0)
                else:
                    lax.fori_loop(0, nk, one, 0)
            return carry

        lax.fori_loop(0, part // PACK, step, 0)

    def arrive(it, n):
        keep(it, n).wait()
        for j in range(1, nk):
            homeward(it, n, j).wait_recv()

    def renew(it, i, t, result):
        for x in range(2):
            r = slice((2 * t + x) * tile, (2 * t + x + 1) * tile)
            total = start[i, x, t].astype(jnp.float32) + back[it, i, r, :].astype(jnp.float32)
            result[i, x, t] = total.astype(jnp.bfloat16)

    for it in range(ITERS):
        if it == 0:
            for i in range(energies):
                for load in loads[i]:
                    load.wait()
                for t in range(tiles):
                    project(i, t, start)
                onsite(it, i, 0)
                if i == 0:
                    pl.semaphore_wait(
                        barrier, nk - 1 + has_near.astype(jnp.int32) + has_far.astype(jnp.int32))
                send(it, i)
        else:
            for n, (t, first, width) in enumerate(home_pieces):
                arrive(it - 1, n)
                for i in range(first, first + width):
                    renew(it - 1, i, t, sigma.at[it - 1])
                    project(i, t, sigma.at[it - 1])
            for i in range(energies):
                onsite(it, i, 0)
                send(it, i)
        for n in range(energies, len(out_pieces)):
            t = out_pieces[n][0]
            for i in range(energies):
                onsite(it, i, t)
            send(it, n)
        if it == 0:
            prepare()
        for c in range(chunks + 1):
            for n, (piece, _, _) in enumerate(out_pieces):
                if piece == c:
                    mine(it, n).wait()
                    for j in range(1, nk):
                        outward(it, n, j).wait_recv()
            if c < chunks:
                @pl.when(has_far)
                def _():
                    halo(it, c, 1).start()

                @pl.when(has_near)
                def _():
                    halo(it, c, 0).start()
            if c > 0:
                @pl.when(has_near)
                def _():
                    halo(it, c - 1, 0).wait_recv()

                @pl.when(has_far)
                def _():
                    halo(it, c - 1, 1).wait_recv()

                for n, (piece, first, width) in enumerate(home_pieces):
                    if piece == c - 1:
                        mix(it, piece, first, width)
                        for j in range(1, nk):
                            homeward(it, n, j).start()
                        keep(it, n).start(priority=1)

    for n, (t, first, width) in enumerate(home_pieces):
        arrive(ITERS - 1, n)
        for i in range(first, first + width):
            renew(ITERS - 1, i, t, sigma_out)
    for it in range(ITERS):
        for n in range(len(out_pieces)):
            for j in range(1, nk):
                outward(it, n, j).wait_send()
                homeward(it, n, j).wait_send()
        for c in range(chunks):
            @pl.when(has_near)
            def _():
                halo(it, c, 0).wait_send()

            @pl.when(has_far)
            def _():
                halo(it, c, 1).wait_send()


def write(*refs):
    count = (len(refs) - 1) // 2
    copies = [pltpu.make_async_copy(refs[i], refs[count + i], refs[-1].at[i]) for i in range(count)]
    for copy in copies:
        copy.start()
    for copy in copies:
        copy.wait()


def body(ne, nk, green, contact, counts, offsets, pairs, table):
    energies, order = green.shape[0], green.shape[-1]
    tile = contact.shape[-1]
    height = contact.shape[2] * contact.shape[3] * tile
    rows = height // nk
    chunks = contact.shape[3]
    pieces = energies + chunks - 1
    blocks = green.reshape(energies, 2, order, order)
    parted = contact.reshape((energies,) + contact.shape[2:])
    flat = jax.ShapeDtypeStruct((energies, height, tile), contact.dtype)
    half = jnp.bfloat16
    result = jax.ShapeDtypeStruct(parted.shape, half)
    dma = pltpu.SemaphoreType.DMA
    anywhere = pl.BlockSpec(memory_space=pl.ANY)
    far = pl.BlockSpec(memory_space=pltpu.HBM)
    near = pl.BlockSpec(memory_space=pltpu.VMEM)
    scalars = pl.BlockSpec(memory_space=pltpu.SMEM)
    results = pl.pallas_call(
        functools.partial(born, ne, nk),
        out_shape=(pltpu.VMEM(parted.shape, half),) * 2,
        in_specs=[far] * 2 + [scalars] * 4,
        out_specs=(near, near),
        scratch_shapes=[
            pltpu.VMEM(blocks.shape, half),
            pltpu.VMEM(parted.shape, half),
            pltpu.VMEM(blocks.shape, half),
            pltpu.VMEM((ITERS,) + flat.shape, half),
            pltpu.VMEM((ITERS, 3, energies, nk, rows, tile), half),
            pltpu.VMEM((ITERS, nk, energies, rows, tile), half),
            pltpu.VMEM((ITERS,) + flat.shape, half),
            pltpu.VMEM((ITERS - 1,) + parted.shape, half),
            pltpu.VMEM((OMAX, nk, nk, 8, tile), jnp.float32),
            dma((2, energies)),
            dma((ITERS, 2, pieces)),
            dma((ITERS, pieces, nk)),
            dma((ITERS, pieces, nk)),
            dma((ITERS, chunks, 2)),
            dma((ITERS, chunks, 2)),
            dma((ITERS, pieces, nk)),
            dma((ITERS, pieces, nk)),
        ],
        compiler_params=pltpu.CompilerParams(
            collective_id=0, has_side_effects=True, vmem_limit_bytes=56 * 2**20
        ),
    )(blocks, parted, counts, offsets, pairs, table)
    lesser, sigma = pl.pallas_call(
        write,
        out_shape=(result, result),
        in_specs=[near] * 2,
        out_specs=(anywhere, anywhere),
        scratch_shapes=[dma((2,))],
        compiler_params=pltpu.CompilerParams(vmem_limit_bytes=4 * 2**20),
    )(*results)
    return lesser.reshape(contact.shape), sigma.reshape(contact.shape)


def solution(mesh):
    blocks = P("energy", "momentum", None, None, None)
    tiles = P("energy", "momentum", None, None, None, None)
    run = functools.partial(body, mesh.shape["energy"], mesh.shape["momentum"])
    return jax.shard_map(run, mesh=mesh, in_specs=(blocks, tiles, P("energy"), P(), P(), P()),
                         out_specs=(tiles, tiles), check_vma=False)
```

```python
import functools
import math

import jax
import jax.numpy as jnp
from jax import lax
from jax.experimental import pallas as pl
from jax.experimental.pallas import tpu as pltpu
from jax.sharding import PartitionSpec as P

OMAX = 3
ITERS = 2
PACK = 16
MESH = pl.DeviceIdType.MESH


def born(ne, nk, green, contact, counts, offsets, pairs, table, lesser_out, sigma_out,
         g, start, product, lesser, band, mixed, back, sigma, weights,
         in_sem, own_sem, a_send, a_recv, h_send, h_recv, b_send, b_recv):
    energies, order = g.shape[0], g.shape[-1]
    tile = start.shape[-1]
    tiles = order // tile
    rows = band.shape[4]
    chunks = tiles
    part = rows // chunks
    modes = offsets.shape[0]
    e, me = lax.axis_index("energy"), lax.axis_index("momentum")
    odd = lax.rem(e, 2)
    near, far = e + 1 - 2 * odd, e - 1 + 2 * odd
    has_near, has_far = near < ne, (far >= 0) & (far < ne)

    loads = []
    for i in range(energies):
        loads.append((pltpu.make_async_copy(contact.at[i], start.at[i], in_sem.at[0, i]),
                      pltpu.make_async_copy(green.at[i], g.at[i], in_sem.at[1, i])))
        for load in loads[i]:
            load.start()

    out_pieces = [(0, i, 1) for i in range(energies)] + [(c, 0, energies) for c in range(1, chunks)]
    home_pieces = [(c, 0, energies) for c in range(chunks - 1)]
    home_pieces += [(chunks - 1, i, 1) for i in range(energies)]

    side = math.isqrt(nk)

    def peer(j):
        if side * side != nk:
            return lax.rem(me + j, nk)
        high, low = j // side, j % side
        high, low = high + odd * (low - high), low + odd * (high - low)
        return lax.rem(me // side + high, side) * side + lax.rem(me % side + low, side)

    barrier = pltpu.get_barrier_semaphore()
    for j in range(1, nk):
        pl.semaphore_signal(barrier, inc=1, device_id={"momentum": peer(j)}, device_id_type=MESH)

    @pl.when(has_near)
    def _():
        pl.semaphore_signal(barrier, inc=1, device_id={"energy": near}, device_id_type=MESH)

    @pl.when(has_far)
    def _():
        pl.semaphore_signal(barrier, inc=1, device_id={"energy": far}, device_id_type=MESH)

    def weigh(i, carry):
        k, q = i // nk, i % nk
        sums = [jnp.float32(0)] * OMAX
        for m in range(modes):
            value = table[m, pairs[m, k, q]]
            for d in range(OMAX):
                sums[d] = sums[d] + jnp.where(offsets[m] == d + 1, value, jnp.float32(0))
        for d in range(OMAX):
            weights[d, k, q] = jnp.full(weights.shape[3:], sums[d], jnp.float32)
        return carry

    def clear(side):
        for it in range(ITERS):
            for i in range(energies):
                def zero(q, carry):
                    band[it, side, i, q] = jnp.zeros(band.shape[4:], band.dtype)
                    return carry
                lax.fori_loop(0, nk, zero, 0)

    def prepare():
        lax.fori_loop(0, nk * nk, weigh, 0)

        @pl.when(e == 0)
        def _():
            clear(0)

        @pl.when(e == ne - 1)
        def _():
            clear(2)

    def project(i, t, source):
        cols = slice(t * tile, (t + 1) * tile)
        s_real, s_imag = source[i, 0, t], source[i, 1, t]
        s = jnp.concatenate([jnp.concatenate([s_real, s_imag], 1),
                             jnp.concatenate([-s_imag, s_real], 1)], 0)
        a = jnp.concatenate([g[i, 0, :, cols], g[i, 1, :, cols]], 1)
        p = jnp.dot(a, s, preferred_element_type=jnp.float32).astype(jnp.bfloat16)
        product[i, 0, :, cols] = p[:, :tile]
        product[i, 1, :, cols] = p[:, tile:]

    def onsite(it, i, t):
        r = slice(t * tile, (t + 1) * tile)
        p = jnp.concatenate([product[i, 0, r, :], product[i, 1, r, :]], 0)
        h = jnp.concatenate([g[i, 0, r, :], g[i, 1, r, :]], 0)
        o = lax.dot_general(p, h, (((1,), (1,)), ((), ())), preferred_element_type=jnp.float32)
        live = jnp.where(t < counts[i], jnp.float32(1), jnp.float32(0))
        real = ((o[:tile, :tile] + o[tile:, tile:]) * live).astype(jnp.bfloat16)
        imag = ((o[tile:, :tile] - o[:tile, tile:]) * live).astype(jnp.bfloat16)
        lesser[it, i, 2 * t * tile:(2 * t + 1) * tile, :] = real
        lesser[it, i, (2 * t + 1) * tile:(2 * t + 2) * tile, :] = imag
        if it == ITERS - 1:
            lesser_out[i, 0, t] = real
            lesser_out[i, 1, t] = imag

    def span(owner, c):
        return pl.ds(pl.multiple_of(c * 2 * tile + owner * part, PACK), part)

    def outward(it, n, j):
        c, i, w = out_pieces[n]
        return pltpu.make_async_remote_copy(
            src_ref=lesser.at[it, pl.ds(i, w), span(peer(j), c), :],
            dst_ref=band.at[it, 1, pl.ds(i, w), me, pl.ds(c * part, part), :],
            send_sem=a_send.at[it, n, j], recv_sem=a_recv.at[it, n, j],
            device_id={"momentum": peer(j)}, device_id_type=MESH)

    def mine(it, n):
        c, i, w = out_pieces[n]
        return pltpu.make_async_copy(lesser.at[it, pl.ds(i, w), span(me, c), :],
                                     band.at[it, 1, pl.ds(i, w), me, pl.ds(c * part, part), :],
                                     own_sem.at[it, 0, n])

    def send(it, n):
        for j in range(1, nk):
            outward(it, n, j).start()
        mine(it, n).start(priority=1)

    def halo(it, c, i, step):
        to = (near, far)[step]
        return pltpu.make_async_remote_copy(
            src_ref=band.at[it, 1, i, :, pl.ds(c * part, part), :],
            dst_ref=band.at[it, 1 + e - to, i, :, pl.ds(c * part, part), :],
            send_sem=h_send.at[it, c, i, step], recv_sem=h_recv.at[it, c, i, step],
            device_id={"energy": to}, device_id_type=MESH)

    def homeward(it, n, j):
        c, i, w = home_pieces[n]
        return pltpu.make_async_remote_copy(
            src_ref=mixed.at[it, peer(j), pl.ds(i, w), pl.ds(c * part, part), :],
            dst_ref=back.at[it, pl.ds(i, w), span(me, c), :],
            send_sem=b_send.at[it, n, j], recv_sem=b_recv.at[it, n, j],
            device_id={"momentum": peer(j)}, device_id_type=MESH)

    def keep(it, n):
        c, i, w = home_pieces[n]
        return pltpu.make_async_copy(mixed.at[it, me, pl.ds(i, w), pl.ds(c * part, part), :],
                                     back.at[it, pl.ds(i, w), span(me, c), :], own_sem.at[it, 1, n])

    def mix(it, c, first, width):
        def step(n, carry):
            r = pl.ds(pl.multiple_of(c * part + n * PACK, PACK), PACK)

            def at(i, q):
                side, i = (0, i + energies) if i < 0 else (1, i) if i < energies else (2, i - energies)
                return band[it, side, i, q, r, :].astype(jnp.float32).reshape(2, PACK // 2, tile)

            for i in range(first, first + width):
                pair = [[at(i - d, q) + at(i + d, q) for q in range(nk)] for d in range(1, OMAX + 1)]

                def one(k, inner):
                    total = None
                    for d in range(OMAX):
                        for q in range(nk):
                            term = weights[d, k, q][None] * pair[d][q]
                            total = term if total is None else total + term
                    mixed[it, k, i, r, :] = total.reshape(PACK, tile).astype(jnp.bfloat16)
                    return inner

                if nk <= 4:
                    for k in range(nk):
                        one(k, 0)
                else:
                    lax.fori_loop(0, nk, one, 0)
            return carry

        lax.fori_loop(0, part // PACK, step, 0)

    def arrive(it, n):
        keep(it, n).wait()
        for j in range(1, nk):
            homeward(it, n, j).wait_recv()

    def renew(it, i, t, result):
        for x in range(2):
            r = slice((2 * t + x) * tile, (2 * t + x + 1) * tile)
            total = start[i, x, t].astype(jnp.float32) + back[it, i, r, :].astype(jnp.float32)
            result[i, x, t] = total.astype(jnp.bfloat16)

    for it in range(ITERS):
        if it == 0:
            for i in range(energies):
                for load in loads[i]:
                    load.wait()
                for t in range(tiles):
                    project(i, t, start)
                onsite(it, i, 0)
                if i == 0:
                    pl.semaphore_wait(
                        barrier, nk - 1 + has_near.astype(jnp.int32) + has_far.astype(jnp.int32))
                send(it, i)
        else:
            for n, (t, first, width) in enumerate(home_pieces):
                arrive(it - 1, n)
                for i in range(first, first + width):
                    renew(it - 1, i, t, sigma.at[it - 1])
                    project(i, t, sigma.at[it - 1])
            for i in range(energies):
                onsite(it, i, 0)
                send(it, i)
        for n in range(energies, len(out_pieces)):
            t = out_pieces[n][0]
            for i in range(energies):
                onsite(it, i, t)
            send(it, n)
        if it == 0:
            prepare()
        for c in range(chunks + 1):
            for n, (piece, first, width) in enumerate(out_pieces):
                if piece == c:
                    mine(it, n).wait()
                    for j in range(1, nk):
                        outward(it, n, j).wait_recv()

                    @pl.when(has_far)
                    def _():
                        for i in range(first, first + width):
                            halo(it, c, i, 1).start()

                    @pl.when(has_near)
                    def _():
                        for i in range(first, first + width):
                            halo(it, c, i, 0).start()
            if c > 0:
                @pl.when(has_near)
                def _():
                    for i in range(energies):
                        halo(it, c - 1, i, 0).wait_recv()

                @pl.when(has_far)
                def _():
                    for i in range(energies):
                        halo(it, c - 1, i, 1).wait_recv()

                for n, (piece, first, width) in enumerate(home_pieces):
                    if piece == c - 1:
                        mix(it, piece, first, width)
                        for j in range(1, nk):
                            homeward(it, n, j).start()
                        keep(it, n).start(priority=1)

    for n, (t, first, width) in enumerate(home_pieces):
        arrive(ITERS - 1, n)
        for i in range(first, first + width):
            renew(ITERS - 1, i, t, sigma_out)
    for it in range(ITERS):
        for n in range(len(out_pieces)):
            for j in range(1, nk):
                outward(it, n, j).wait_send()
                homeward(it, n, j).wait_send()
        for c in range(chunks):
            @pl.when(has_near)
            def _():
                for i in range(energies):
                    halo(it, c, i, 0).wait_send()

            @pl.when(has_far)
            def _():
                for i in range(energies):
                    halo(it, c, i, 1).wait_send()


def write(*refs):
    count = (len(refs) - 1) // 2
    copies = [pltpu.make_async_copy(refs[i], refs[count + i], refs[-1].at[i]) for i in range(count)]
    for copy in copies:
        copy.start()
    for copy in copies:
        copy.wait()


def body(ne, nk, green, contact, counts, offsets, pairs, table):
    energies, order = green.shape[0], green.shape[-1]
    tile = contact.shape[-1]
    height = contact.shape[2] * contact.shape[3] * tile
    rows = height // nk
    chunks = contact.shape[3]
    pieces = energies + chunks - 1
    blocks = green.reshape(energies, 2, order, order)
    parted = contact.reshape((energies,) + contact.shape[2:])
    flat = jax.ShapeDtypeStruct((energies, height, tile), contact.dtype)
    half = jnp.bfloat16
    result = jax.ShapeDtypeStruct(parted.shape, half)
    dma = pltpu.SemaphoreType.DMA
    anywhere = pl.BlockSpec(memory_space=pl.ANY)
    far = pl.BlockSpec(memory_space=pltpu.HBM)
    near = pl.BlockSpec(memory_space=pltpu.VMEM)
    scalars = pl.BlockSpec(memory_space=pltpu.SMEM)
    results = pl.pallas_call(
        functools.partial(born, ne, nk),
        out_shape=(pltpu.VMEM(parted.shape, half),) * 2,
        in_specs=[far] * 2 + [scalars] * 4,
        out_specs=(near, near),
        scratch_shapes=[
            pltpu.VMEM(blocks.shape, half),
            pltpu.VMEM(parted.shape, half),
            pltpu.VMEM(blocks.shape, half),
            pltpu.VMEM((ITERS,) + flat.shape, half),
            pltpu.VMEM((ITERS, 3, energies, nk, rows, tile), half),
            pltpu.VMEM((ITERS, nk, energies, rows, tile), half),
            pltpu.VMEM((ITERS,) + flat.shape, half),
            pltpu.VMEM((ITERS - 1,) + parted.shape, half),
            pltpu.VMEM((OMAX, nk, nk, 8, tile), jnp.float32),
            dma((2, energies)),
            dma((ITERS, 2, pieces)),
            dma((ITERS, pieces, nk)),
            dma((ITERS, pieces, nk)),
            dma((ITERS, chunks, energies, 2)),
            dma((ITERS, chunks, energies, 2)),
            dma((ITERS, pieces, nk)),
            dma((ITERS, pieces, nk)),
        ],
        compiler_params=pltpu.CompilerParams(
            collective_id=0, has_side_effects=True, vmem_limit_bytes=56 * 2**20
        ),
    )(blocks, parted, counts, offsets, pairs, table)
    lesser, sigma = pl.pallas_call(
        write,
        out_shape=(result, result),
        in_specs=[near] * 2,
        out_specs=(anywhere, anywhere),
        scratch_shapes=[dma((2,))],
        compiler_params=pltpu.CompilerParams(vmem_limit_bytes=4 * 2**20),
    )(*results)
    return lesser.reshape(contact.shape), sigma.reshape(contact.shape)


def solution(mesh):
    blocks = P("energy", "momentum", None, None, None)
    tiles = P("energy", "momentum", None, None, None, None)
    run = functools.partial(body, mesh.shape["energy"], mesh.shape["momentum"])
    return jax.shard_map(run, mesh=mesh, in_specs=(blocks, tiles, P("energy"), P(), P(), P()),
                         out_specs=(tiles, tiles), check_vma=False)
```

```python
import functools

import jax
import jax.numpy as jnp
from jax import lax
from jax.experimental import pallas as pl
from jax.experimental.pallas import tpu as pltpu
from jax.sharding import PartitionSpec as P

OMAX = 3
ITERS = 2
PACK = 16
MESH = pl.DeviceIdType.MESH


def born(ne, nk, green, contact, counts, offsets, pairs, table, lesser_out, sigma_out,
         g, start, product, lesser, band, mixed, back, sigma, weights,
         in_sem, own_sem, a_send, a_recv, h_send, h_recv, b_send, b_recv):
    energies, order = g.shape[0], g.shape[-1]
    tile = start.shape[-1]
    tiles = order // tile
    rows = band.shape[4]
    chunks = tiles
    part = rows // chunks
    modes = offsets.shape[0]
    e, me = lax.axis_index("energy"), lax.axis_index("momentum")
    odd = lax.rem(e, 2)
    near, far = e + 1 - 2 * odd, e - 1 + 2 * odd
    has_near, has_far = near < ne, (far >= 0) & (far < ne)

    loads = []
    for i in range(energies):
        loads.append((pltpu.make_async_copy(contact.at[i], start.at[i], in_sem.at[0, i]),
                      pltpu.make_async_copy(green.at[i], g.at[i], in_sem.at[1, i])))
        for load in loads[i]:
            load.start()

    out_pieces = [(0, i, 1) for i in range(energies)] + [(c, 0, energies) for c in range(1, chunks)]
    home_pieces = [(c, 0, energies) for c in range(chunks - 1)]
    home_pieces += [(chunks - 1, i, 1) for i in range(energies)]

    def peer(j):
        return lax.rem(me + j, nk)

    barrier = pltpu.get_barrier_semaphore()
    for j in range(1, nk):
        pl.semaphore_signal(barrier, inc=1, device_id={"momentum": peer(j)}, device_id_type=MESH)

    @pl.when(has_near)
    def _():
        pl.semaphore_signal(barrier, inc=1, device_id={"energy": near}, device_id_type=MESH)

    @pl.when(has_far)
    def _():
        pl.semaphore_signal(barrier, inc=1, device_id={"energy": far}, device_id_type=MESH)

    def weigh(i, carry):
        k, q = i // nk, i % nk
        sums = [jnp.float32(0)] * OMAX
        for m in range(modes):
            value = table[m, pairs[m, k, q]]
            for d in range(OMAX):
                sums[d] = sums[d] + jnp.where(offsets[m] == d + 1, value, jnp.float32(0))
        for d in range(OMAX):
            weights[d, k, q] = jnp.full(weights.shape[3:], sums[d], jnp.float32)
        return carry

    def clear(side):
        for it in range(ITERS):
            for i in range(energies):
                def zero(q, carry):
                    band[it, side, i, q] = jnp.zeros(band.shape[4:], band.dtype)
                    return carry
                lax.fori_loop(0, nk, zero, 0)

    def prepare():
        lax.fori_loop(0, nk * nk, weigh, 0)

        @pl.when(e == 0)
        def _():
            clear(0)

        @pl.when(e == ne - 1)
        def _():
            clear(2)

    def project(i, t, source):
        cols = slice(t * tile, (t + 1) * tile)
        s_real, s_imag = source[i, 0, t], source[i, 1, t]
        s = jnp.concatenate([jnp.concatenate([s_real, s_imag], 1),
                             jnp.concatenate([-s_imag, s_real], 1)], 0)
        a = jnp.concatenate([g[i, 0, :, cols], g[i, 1, :, cols]], 1)
        p = jnp.dot(a, s, preferred_element_type=jnp.float32).astype(jnp.bfloat16)
        product[i, 0, :, cols] = p[:, :tile]
        product[i, 1, :, cols] = p[:, tile:]

    def onsite(it, i, t):
        r = slice(t * tile, (t + 1) * tile)
        p = jnp.concatenate([product[i, 0, r, :], product[i, 1, r, :]], 0)
        h = jnp.concatenate([g[i, 0, r, :], g[i, 1, r, :]], 0)
        o = lax.dot_general(p, h, (((1,), (1,)), ((), ())), preferred_element_type=jnp.float32)
        live = jnp.where(t < counts[i], jnp.float32(1), jnp.float32(0))
        real = ((o[:tile, :tile] + o[tile:, tile:]) * live).astype(jnp.bfloat16)
        imag = ((o[tile:, :tile] - o[:tile, tile:]) * live).astype(jnp.bfloat16)
        lesser[it, i, 2 * t * tile:(2 * t + 1) * tile, :] = real
        lesser[it, i, (2 * t + 1) * tile:(2 * t + 2) * tile, :] = imag
        if it == ITERS - 1:
            lesser_out[i, 0, t] = real
            lesser_out[i, 1, t] = imag

    def span(owner, c):
        return pl.ds(pl.multiple_of(c * 2 * tile + owner * part, PACK), part)

    def outward(it, n, j):
        c, i, w = out_pieces[n]
        return pltpu.make_async_remote_copy(
            src_ref=lesser.at[it, pl.ds(i, w), span(peer(j), c), :],
            dst_ref=band.at[it, 1, pl.ds(i, w), me, pl.ds(c * part, part), :],
            send_sem=a_send.at[it, n, j], recv_sem=a_recv.at[it, n, j],
            device_id={"momentum": peer(j)}, device_id_type=MESH)

    def mine(it, n):
        c, i, w = out_pieces[n]
        return pltpu.make_async_copy(lesser.at[it, pl.ds(i, w), span(me, c), :],
                                     band.at[it, 1, pl.ds(i, w), me, pl.ds(c * part, part), :],
                                     own_sem.at[it, 0, n])

    def send(it, n):
        for j in range(1, nk):
            outward(it, n, j).start()
        mine(it, n).start(priority=1)

    def halo(it, c, i, step):
        to = (near, far)[step]
        return pltpu.make_async_remote_copy(
            src_ref=band.at[it, 1, i, :, pl.ds(c * part, part), :],
            dst_ref=band.at[it, 1 + e - to, i, :, pl.ds(c * part, part), :],
            send_sem=h_send.at[it, c, i, step], recv_sem=h_recv.at[it, c, i, step],
            device_id={"energy": to}, device_id_type=MESH)

    def homeward(it, n, j):
        c, i, w = home_pieces[n]
        return pltpu.make_async_remote_copy(
            src_ref=mixed.at[it, peer(j), pl.ds(i, w), pl.ds(c * part, part), :],
            dst_ref=back.at[it, pl.ds(i, w), span(me, c), :],
            send_sem=b_send.at[it, n, j], recv_sem=b_recv.at[it, n, j],
            device_id={"momentum": peer(j)}, device_id_type=MESH)

    def keep(it, n):
        c, i, w = home_pieces[n]
        return pltpu.make_async_copy(mixed.at[it, me, pl.ds(i, w), pl.ds(c * part, part), :],
                                     back.at[it, pl.ds(i, w), span(me, c), :], own_sem.at[it, 1, n])

    def mix(it, c, first, width):
        def step(n, carry):
            r = pl.ds(pl.multiple_of(c * part + n * PACK, PACK), PACK)

            def at(i, q):
                side, i = (0, i + energies) if i < 0 else (1, i) if i < energies else (2, i - energies)
                return band[it, side, i, q, r, :].astype(jnp.float32).reshape(2, PACK // 2, tile)

            for i in range(first, first + width):
                pair = [[at(i - d, q) + at(i + d, q) for q in range(nk)] for d in range(1, OMAX + 1)]

                def one(k, inner):
                    total = None
                    for d in range(OMAX):
                        for q in range(nk):
                            term = weights[d, k, q][None] * pair[d][q]
                            total = term if total is None else total + term
                    mixed[it, k, i, r, :] = total.reshape(PACK, tile).astype(jnp.bfloat16)
                    return inner

                if nk <= 4:
                    for k in range(nk):
                        one(k, 0)
                else:
                    lax.fori_loop(0, nk, one, 0)
            return carry

        lax.fori_loop(0, part // PACK, step, 0)

    def arrive(it, n):
        keep(it, n).wait()
        for j in range(1, nk):
            homeward(it, n, j).wait_recv()

    def renew(it, i, t, result):
        for x in range(2):
            r = slice((2 * t + x) * tile, (2 * t + x + 1) * tile)
            total = start[i, x, t].astype(jnp.float32) + back[it, i, r, :].astype(jnp.float32)
            result[i, x, t] = total.astype(jnp.bfloat16)

    for it in range(ITERS):
        if it == 0:
            for i in range(energies):
                for load in loads[i]:
                    load.wait()
                for t in range(tiles):
                    project(i, t, start)
                onsite(it, i, 0)
                if i == 0:
                    pl.semaphore_wait(
                        barrier, nk - 1 + has_near.astype(jnp.int32) + has_far.astype(jnp.int32))
                send(it, i)
        else:
            for n, (t, first, width) in enumerate(home_pieces):
                arrive(it - 1, n)
                for i in range(first, first + width):
                    renew(it - 1, i, t, sigma.at[it - 1])
                    project(i, t, sigma.at[it - 1])
            for i in range(energies):
                onsite(it, i, 0)
                send(it, i)
        for n in range(energies, len(out_pieces)):
            t = out_pieces[n][0]
            for i in range(energies):
                onsite(it, i, t)
            send(it, n)
        if it == 0:
            prepare()
        for c in range(chunks + 1):
            for n, (piece, first, width) in enumerate(out_pieces):
                if piece == c:
                    mine(it, n).wait()
                    for j in range(1, nk):
                        outward(it, n, j).wait_recv()

                    @pl.when(has_far)
                    def _():
                        for i in range(first, first + width):
                            halo(it, c, i, 1).start()

                    @pl.when(has_near)
                    def _():
                        for i in range(first, first + width):
                            halo(it, c, i, 0).start()
            if c > 0:
                @pl.when(has_near)
                def _():
                    for i in range(energies):
                        halo(it, c - 1, i, 0).wait_recv()

                @pl.when(has_far)
                def _():
                    for i in range(energies):
                        halo(it, c - 1, i, 1).wait_recv()

                for n, (piece, first, width) in enumerate(home_pieces):
                    if piece == c - 1:
                        mix(it, piece, first, width)
                        for j in range(1, nk):
                            homeward(it, n, j).start()
                        keep(it, n).start(priority=1)

    for n, (t, first, width) in enumerate(home_pieces):
        arrive(ITERS - 1, n)
        for i in range(first, first + width):
            renew(ITERS - 1, i, t, sigma_out)
    for it in range(ITERS):
        for n in range(len(out_pieces)):
            for j in range(1, nk):
                outward(it, n, j).wait_send()
                homeward(it, n, j).wait_send()
        for c in range(chunks):
            @pl.when(has_near)
            def _():
                for i in range(energies):
                    halo(it, c, i, 0).wait_send()

            @pl.when(has_far)
            def _():
                for i in range(energies):
                    halo(it, c, i, 1).wait_send()


def write(*refs):
    count = (len(refs) - 1) // 2
    copies = [pltpu.make_async_copy(refs[i], refs[count + i], refs[-1].at[i]) for i in range(count)]
    for copy in copies:
        copy.start()
    for copy in copies:
        copy.wait()


def body(ne, nk, green, contact, counts, offsets, pairs, table):
    energies, order = green.shape[0], green.shape[-1]
    tile = contact.shape[-1]
    height = contact.shape[2] * contact.shape[3] * tile
    rows = height // nk
    chunks = contact.shape[3]
    pieces = energies + chunks - 1
    blocks = green.reshape(energies, 2, order, order)
    parted = contact.reshape((energies,) + contact.shape[2:])
    flat = jax.ShapeDtypeStruct((energies, height, tile), contact.dtype)
    half = jnp.bfloat16
    result = jax.ShapeDtypeStruct(parted.shape, half)
    dma = pltpu.SemaphoreType.DMA
    anywhere = pl.BlockSpec(memory_space=pl.ANY)
    far = pl.BlockSpec(memory_space=pltpu.HBM)
    near = pl.BlockSpec(memory_space=pltpu.VMEM)
    scalars = pl.BlockSpec(memory_space=pltpu.SMEM)
    results = pl.pallas_call(
        functools.partial(born, ne, nk),
        out_shape=(pltpu.VMEM(parted.shape, half),) * 2,
        in_specs=[far] * 2 + [scalars] * 4,
        out_specs=(near, near),
        scratch_shapes=[
            pltpu.VMEM(blocks.shape, half),
            pltpu.VMEM(parted.shape, half),
            pltpu.VMEM(blocks.shape, half),
            pltpu.VMEM((ITERS,) + flat.shape, half),
            pltpu.VMEM((ITERS, 3, energies, nk, rows, tile), half),
            pltpu.VMEM((ITERS, nk, energies, rows, tile), half),
            pltpu.VMEM((ITERS,) + flat.shape, half),
            pltpu.VMEM((ITERS - 1,) + parted.shape, half),
            pltpu.VMEM((OMAX, nk, nk, 8, tile), jnp.float32),
            dma((2, energies)),
            dma((ITERS, 2, pieces)),
            dma((ITERS, pieces, nk)),
            dma((ITERS, pieces, nk)),
            dma((ITERS, chunks, energies, 2)),
            dma((ITERS, chunks, energies, 2)),
            dma((ITERS, pieces, nk)),
            dma((ITERS, pieces, nk)),
        ],
        compiler_params=pltpu.CompilerParams(
            collective_id=0, has_side_effects=True, vmem_limit_bytes=56 * 2**20
        ),
    )(blocks, parted, counts, offsets, pairs, table)
    lesser, sigma = pl.pallas_call(
        write,
        out_shape=(result, result),
        in_specs=[near] * 2,
        out_specs=(anywhere, anywhere),
        scratch_shapes=[dma((2,))],
        compiler_params=pltpu.CompilerParams(vmem_limit_bytes=4 * 2**20),
    )(*results)
    return lesser.reshape(contact.shape), sigma.reshape(contact.shape)


def solution(mesh):
    blocks = P("energy", "momentum", None, None, None)
    tiles = P("energy", "momentum", None, None, None, None)
    run = functools.partial(body, mesh.shape["energy"], mesh.shape["momentum"])
    return jax.shard_map(run, mesh=mesh, in_specs=(blocks, tiles, P("energy"), P(), P(), P()),
                         out_specs=(tiles, tiles), check_vma=False)
```
